32 devices in a mesh: dom: 16 (over z, x, core), cls: 2 (over y).
Axes of the slice: x: 2, y: 2, z: 4, core: 2. Of those that a mesh axis runs over, the one named last changes fastest.
Arguments:
- images: bfloat16 [128, 9216], P(('dom', 'cls')), may hold values from -64 to 64
- ctf: float32 [128, 64], P(('dom', 'cls')), may hold values from 0.2 to 1
- inv_noise: float32 [64], replicated, may hold values from 0.5 to 2
- classes: bfloat16 [400, 9216], P('cls'), may hold values from -0.25 to 0.25
- candidates: int32 [128, 2], P(('dom', 'cls')), may hold values from 0 to 399, as said below
Outputs:
- class_sums: float32 [9216, 400], P('dom', 'cls')
- weight_sums: float32 [400, 64], P('cls')
- evidence: float32 [128], P(('dom', 'cls'))
The draws below stay inside these ranges and needn't reach their ends.
Inputs may be any that keep to these rules, and one draw needn't show every extreme that they name: `candidates`: each row names 2 different classes. Among the 4 particles of one device, at most 4 name a class of any one block b (classes b * 200 to (b + 1) * 200 - 1); for each index along dom, the 2 devices that share it have one common block that exactly 4 particles of each of them name.
All inputs are finite; a program needn't handle non-finite values.
Results may differ from the reference program's by a relative error of at most 0.0053.
Values may be sent and summed in bfloat16 or wider, within the bound.
A program may use at most 64 MiB of HBM per device.

```python
import math
import jax
import jax.numpy as jnp
from jax import lax

CYCLES = 64
ANGLES = 72
ROTATIONS = 36
CLASSES = 400
TOP_CAND = 2
PART_DEV = 4
FEATURES = 9216
CLASS_BLOCK = 200
CAPACITY = 4
PARTICLES = 128
N_CLS = 2


def class_values(key):
    scale_key, shell_key, value_key = jax.random.split(jax.random.fold_in(key, 11), 3)
    overall = jnp.exp(jax.random.uniform(scale_key, (CLASSES, 1, 1, 1), jnp.float32, math.log(0.5), math.log(2.0)))
    shells = jnp.exp(jax.random.uniform(shell_key, (CLASSES, 1, 1, CYCLES), jnp.float32, math.log(0.5), math.log(2.0)))
    raw_values = jnp.clip(jax.random.normal(value_key, (CLASSES, ANGLES, 2, CYCLES), jnp.float32), -6.0, 6.0)
    values = raw_values * overall * shells / math.sqrt(FEATURES)
    return values.reshape(CLASSES, FEATURES)


def candidate_ids(key):
    device_total = PARTICLES // PART_DEV

    def one_device(device):
        device_key = jax.random.fold_in(jax.random.fold_in(key, 23), device)
        group_key = jax.random.fold_in(jax.random.fold_in(key, 29), device // N_CLS)
        hot_block = jax.random.randint(group_key, (), 0, N_CLS)
        order_key, slot_key, base_key, extra_key, swap_key = jax.random.split(device_key, 5)
        shuffled = jax.random.permutation(order_key, PART_DEV)
        chosen = jnp.zeros((PART_DEV,), jnp.int32).at[shuffled[:CAPACITY]].set(1)
        pair_index = jnp.arange(PART_DEV * TOP_CAND, dtype=jnp.int32)
        pair_part = pair_index // TOP_CAND
        pair_slot = pair_index % TOP_CAND
        first_hot = (pair_slot == 0) & (chosen[pair_part] == 1)
        remaining = 1 - first_hot.astype(jnp.int32)
        ranking = jnp.clip(jnp.cumsum(remaining) - 1, 0, (N_CLS - 1) * CAPACITY - 1)
        slot_order = jax.random.permutation(slot_key, (N_CLS - 1) * CAPACITY)
        other_block = slot_order[ranking] // CAPACITY
        other_block = other_block + (other_block >= hot_block).astype(jnp.int32)
        owner_block = jnp.where(first_hot, hot_block, other_block)
        base_offset = jax.random.randint(base_key, (PART_DEV,), 0, CLASS_BLOCK)
        extra_offset = jax.random.randint(extra_key, (PART_DEV,), 0, CLASS_BLOCK - 1)
        offsets = jnp.where(pair_slot == 0, base_offset[pair_part], (base_offset[pair_part] + 1 + extra_offset[pair_part]) % CLASS_BLOCK)
        class_ids = (owner_block * CLASS_BLOCK + offsets).reshape(PART_DEV, TOP_CAND)
        swap_flag = jax.random.randint(swap_key, (PART_DEV, 1), 0, 2)
        return jnp.where(swap_flag == 1, class_ids[:, ::-1], class_ids)
    device_ids = jax.vmap(one_device)(jnp.arange(device_total, dtype=jnp.int32))
    return device_ids.reshape(PARTICLES, TOP_CAND).astype(jnp.int32)


def draw_classes(key, part):
    return class_values(key).astype(jnp.bfloat16)


def draw_candidates(key, part):
    return candidate_ids(key)


def draw_images(key, part):
    values = jax.random.normal(jax.random.fold_in(key, 41), (PARTICLES, FEATURES), jnp.float32)
    return jnp.clip(values, -8.0, 8.0).astype(jnp.bfloat16)


def steps_of(stream_key, extent, cuts, low, largest):
    gain = 1.0
    for position, blocks in cuts:
        draws = jax.random.uniform(jax.random.fold_in(jax.random.fold_in(stream_key, 6), position), (blocks,), jnp.float32, low / len(cuts), largest / len(cuts))
        gain = gain * jnp.repeat(jnp.exp(draws), extent[position] // blocks).reshape((-1,) + (1,) * (len(extent) - 1 - position))
    return gain


def setup_inputs(seed: int = 0) -> dict:
    key_list = jax.random.split(jax.random.key(seed), 6)
    return {
        "images": draw_images(jax.random.fold_in(key_list[5], 71), 0),
        "ctf": jnp.clip(0.2 + 0.8 * jax.random.uniform(key_list[1], (PARTICLES, CYCLES), jnp.float32) ** steps_of(key_list[1], (PARTICLES, CYCLES), ((0, 32),), -0.2, 0.2), 0.2, 1.0),
        "inv_noise": jnp.clip(jnp.exp(jax.random.uniform(key_list[2], (CYCLES,), jnp.float32, math.log(0.5), math.log(2.0))), 0.5, 2.0),
        "classes": draw_classes(jax.random.fold_in(key_list[5], 71), 0),
        "candidates": draw_candidates(jax.random.fold_in(key_list[5], 71), 0),
    }


def class_frame(data, rotation):
    shaped = data.reshape(data.shape[0], ANGLES, 2 * CYCLES)
    doubled = jnp.concatenate([shaped, shaped], axis=1)
    start_angle = (rotation * (ANGLES // ROTATIONS)).astype(jnp.int32)
    moved = lax.dynamic_slice_in_dim(doubled, start_angle, ANGLES, 1)
    return moved.reshape(data.shape[0], 2 * CYCLES * ANGLES)


def reference(images, ctf, inv_noise, classes, candidates):
    ctf_noise = ctf * inv_noise[None, :]
    factor = jnp.tile(ctf_noise, (1, 2 * ANGLES))
    weighted = (images.astype(jnp.float32) * factor).astype(jnp.bfloat16)
    quadratic = (ctf * ctf * inv_noise[None, :]).astype(jnp.bfloat16)
    quad_wide = quadratic.astype(jnp.float32)
    class_wide = classes.astype(jnp.float32)
    energy = jnp.sum(jnp.square(class_wide).reshape(CLASSES, 2 * ANGLES, CYCLES), axis=1)
    picked = classes[candidates].astype(jnp.float32)
    norm_term = jnp.einsum("nr,njr->nj", quad_wide, energy[candidates], precision=lax.Precision.HIGHEST)

    def correlate(rotation):
        framed = class_frame(weighted, rotation).astype(jnp.float32)
        return jnp.einsum("nf,njf->nj", framed, picked, precision=lax.Precision.HIGHEST)

    cross = lax.map(correlate, jnp.arange(ROTATIONS, dtype=jnp.int32))
    logits = jnp.transpose(cross, (1, 2, 0)) - 0.5 * norm_term[:, :, None]
    highest = jnp.max(logits, axis=(1, 2))
    totals = jnp.sum(jnp.exp(logits - highest[:, None, None]), axis=(1, 2))
    evidence = highest + jnp.log(totals)
    posterior = jnp.exp(logits - evidence[:, None, None]).astype(jnp.bfloat16)
    post_wide = posterior.astype(jnp.float32)

    def accumulate(carry, rotation):
        framed = class_frame(weighted, rotation).astype(jnp.float32)
        weight_now = lax.dynamic_index_in_dim(post_wide, rotation, 2, keepdims=False)
        return carry + weight_now[:, :, None] * framed[:, None, :], rotation

    start_sums = jnp.zeros((PARTICLES, TOP_CAND, FEATURES), jnp.float32)
    contrib, unused = lax.scan(accumulate, start_sums, jnp.arange(ROTATIONS, dtype=jnp.int32))
    flat_ids = candidates.reshape(-1)
    sums = jax.ops.segment_sum(contrib.reshape(PARTICLES * TOP_CAND, FEATURES), flat_ids, num_segments=CLASSES)
    weight_total = jnp.sum(post_wide, axis=2)
    ctf_terms = weight_total[:, :, None] * quad_wide[:, None, :]
    weight_sums = jax.ops.segment_sum(ctf_terms.reshape(PARTICLES * TOP_CAND, CYCLES), flat_ids, num_segments=CLASSES)
    return (sums.T, weight_sums, evidence)
```

```python
import functools
import math

import jax
import jax.numpy as jnp
from jax import lax
from jax.experimental import pallas as pl
from jax.experimental.pallas import tpu as pltpu
from jax.sharding import PartitionSpec as P

ANGLES = 72
ROTATIONS = 36
TOP_CAND = 2


NEGATIVE = -1e30


def combined_all(value, axis, join):
    pieces = jax.tree.map(lambda part: lax.all_gather(part, axis), value)
    head = jax.tree.map(lambda part: part[0], pieces)
    tail = jax.tree.map(lambda part: part[1:], pieces)
    subtotal, _ = lax.scan(lambda subtotal, section: (join(subtotal, section), None), head, tail)
    return subtotal


def combine_totals(earlier, later):
    highest = jnp.maximum(earlier[0], later[0])
    return (
        highest,
        earlier[1] * jnp.exp(earlier[0] - highest) + later[1] * jnp.exp(later[0] - highest),
    )


def shards(images, ctf, inv_noise, classes, candidates):
    cls_count = lax.axis_size("cls")
    my_index = lax.axis_index("cls")
    part_dev = images.shape[0]
    class_block = classes.shape[0]
    features = images.shape[1]
    cycles = ctf.shape[1]
    capacity = min(5 * part_dev * TOP_CAND // (2 * cls_count), part_dev)
    group_size = cls_count * part_dev
    shift = features // ANGLES * (ANGLES // ROTATIONS)
    turn_ids = jnp.arange(ROTATIONS, dtype=jnp.int32)
    ctf_noise = ctf * inv_noise[None, :]
    weighted = (images.astype(jnp.float32) * jnp.tile(ctf_noise, (1, features // cycles))).astype(
        jnp.bfloat16
    )
    quadratic = (ctf * ctf * inv_noise[None, :]).astype(jnp.bfloat16)
    everyone = lax.all_gather(candidates, "cls", axis=0, tiled=True)
    block_ids = jnp.arange(class_block, dtype=jnp.int32) + my_index * class_block
    cand_mask = jnp.any(everyone[:, :, None] == block_ids[None, None, :], axis=1).astype(
        jnp.float32
    )
    owner_ids = jnp.arange(cls_count, dtype=jnp.int32)
    routed = jnp.any(
        (everyone // class_block)[:, :, None] == owner_ids[None, None, :], axis=1
    ).astype(jnp.int32)
    by_source = routed.reshape(cls_count, part_dev, cls_count)
    slot_of = jnp.cumsum(by_source, axis=1) - by_source
    slot_ids = jnp.arange(capacity, dtype=jnp.int32)
    mine_routed = lax.dynamic_index_in_dim(by_source, my_index, 0, keepdims=False)
    mine_slot = lax.dynamic_index_in_dim(slot_of, my_index, 0, keepdims=False)
    packing = (mine_routed.T[:, None, :] == 1) & (
        mine_slot.T[:, None, :] == slot_ids[None, :, None]
    )
    packing = packing.reshape(cls_count * capacity, part_dev).astype(jnp.bfloat16)
    send_data = jnp.dot(packing, weighted, preferred_element_type=jnp.float32).astype(jnp.bfloat16)
    send_quad = jnp.dot(packing, quadratic, preferred_element_type=jnp.float32).astype(jnp.bfloat16)
    row_data, row_quad = (
        lax.all_to_all(send_data, "cls", split_axis=0, concat_axis=0, tiled=True),
        lax.all_to_all(send_quad, "cls", split_axis=0, concat_axis=0, tiled=True),
    )
    into_mine = lax.dynamic_index_in_dim(by_source, my_index, 2, keepdims=False)
    slot_mine = lax.dynamic_index_in_dim(slot_of, my_index, 2, keepdims=False)
    selected = (into_mine[:, None, :] == 1) & (slot_mine[:, None, :] == slot_ids[None, :, None])
    diagonal = jnp.eye(cls_count, dtype=jnp.float32)
    unpack = (selected.astype(jnp.float32)[:, :, None, :] * diagonal[:, None, :, None]).reshape(
        cls_count * capacity, group_size
    )
    row_mask = jnp.dot(unpack, cand_mask, precision=lax.Precision.HIGHEST)
    row_count = row_data.shape[0]
    energy = jnp.sum(
        jnp.square(classes.astype(jnp.float32)).reshape(class_block, features // cycles, cycles),
        axis=1,
    )
    quad_wide = row_quad.astype(jnp.float32)
    norm_term = jnp.dot(quad_wide, energy.T, precision=lax.Precision.HIGHEST)
    twin_classes = jnp.concatenate([classes, classes], axis=1)
    feat_block = math.gcd(features, 1152)

    def add_block(block_index, running):
        offset = block_index * feat_block
        rotated = jax.vmap(
            lambda rotation: lax.dynamic_slice_in_dim(
                twin_classes, offset - rotation * shift + features, feat_block, 1
            )
        )(turn_ids)
        section = lax.dynamic_slice_in_dim(row_data, offset, feat_block, 1)
        return running + lax.dot_general(
            section, rotated, (((1,), (2,)), ((), ())), preferred_element_type=jnp.float32
        )

    cross = lax.fori_loop(
        0,
        features // feat_block,
        add_block,
        jnp.zeros((row_count, ROTATIONS, class_block), jnp.float32),
    )
    logits = cross - 0.5 * norm_term[:, None, :]
    live = jnp.broadcast_to(row_mask[:, None, :] > 0.5, logits.shape)
    masked = jnp.where(live, logits, NEGATIVE)
    peak = jnp.max(masked, axis=(1, 2))
    part_total = jnp.sum(jnp.where(live, jnp.exp(masked - peak[:, None, None]), 0.0), axis=(1, 2))
    group_peak = jnp.max(jnp.where(unpack > 0.5, peak[:, None], NEGATIVE), axis=0)
    group_total = jnp.sum(unpack * part_total[:, None], axis=0)
    top_all, total_all = combined_all((group_peak, group_total), "cls", combine_totals)
    group_evidence = top_all + jnp.log(total_all)
    own_evidence = lax.dynamic_slice_in_dim(group_evidence, my_index * part_dev, part_dev, 0)
    row_evidence = jnp.dot(unpack, group_evidence, precision=lax.Precision.HIGHEST)
    posterior = jnp.where(live, jnp.exp(logits - row_evidence[:, None, None]), 0.0).astype(
        jnp.bfloat16
    )
    weight_total = jnp.sum(posterior.astype(jnp.float32), axis=1)
    ctf_part = jnp.dot(weight_total.T, quad_wide, precision=lax.Precision.HIGHEST)
    weight_sums = lax.psum(ctf_part, "dom")
    twin_rows = jnp.concatenate([row_data, row_data], axis=1)

    def add_sums(block_index, running):
        offset = block_index * feat_block
        stacked = jax.vmap(
            lambda rotation: lax.dynamic_slice_in_dim(
                twin_rows, offset + rotation * shift, feat_block, 1
            )
        )(turn_ids)
        block_sum = lax.dot_general(
            posterior, stacked, (((0, 1), (1, 0)), ((), ())), preferred_element_type=jnp.float32
        )
        return lax.dynamic_update_slice_in_dim(running, block_sum, offset, 1)

    summed = lax.fori_loop(
        0, features // feat_block, add_sums, jnp.zeros((class_block, features), jnp.float32)
    )
    full_term = summed.T
    class_sums = lax.psum_scatter(full_term, "dom", scatter_dimension=0, tiled=True)
    return (class_sums, weight_sums, own_evidence)


MESH = pl.DeviceIdType.MESH
LANES = 128


def estep_kernel(
    doms,
    images_ref,
    ctf_ref,
    noise_ref,
    cand_ref,
    classes_ref,
    sums_ref,
    weight_ref,
    evidence_ref,
    held,
    own_wide,
    own_send,
    other_recv,
    other_wide,
    group_wide,
    twin_even,
    twin_odd,
    framed,
    part_send,
    part_recv,
    ids_send,
    ids_recv,
    stage,
    arrived,
    load_sem,
    pair_send_sem,
    pair_recv_sem,
    ids_send_sem,
    ids_recv_sem,
    data_send_sem,
    data_recv_sem,
):
    me = lax.axis_index("dom")
    side = lax.axis_index("cls")
    part_dev, features = images_ref.shape
    cycles = ctf_ref.shape[1]
    class_block = held.shape[0]
    shift = framed.shape[1] // ROTATIONS
    group = 2 * part_dev
    rows = ROTATIONS * group
    pairs = TOP_CAND * group
    own_rows = ROTATIONS * part_dev
    share = features // doms
    wide = stage.shape[1]
    peers = [lax.rem(me + step, doms) for step in range(1, doms)]

    load = pltpu.make_async_copy(classes_ref, held, load_sem)
    load.start()
    barrier = pltpu.get_barrier_semaphore()
    pl.semaphore_signal(barrier, inc=1, device_id={"cls": 1 - side}, device_id_type=MESH)
    for peer in peers:
        pl.semaphore_signal(barrier, inc=1, device_id={"dom": peer}, device_id_type=MESH)

    ctf = ctf_ref[...]
    noise = noise_ref[...]
    factor = jnp.concatenate([ctf * noise] * (shift // cycles), axis=1)
    quad = (ctf * ctf * noise).astype(jnp.bfloat16).astype(jnp.float32)
    cand = cand_ref[...]

    def local_ids(block, column):
        local = cand[:, column : column + 1] - block * class_block
        inside = (local >= 0) & (local < class_block)
        local = jnp.where(inside, local, -1).astype(jnp.float32)
        return jnp.broadcast_to(local, (part_dev, cycles))

    def extras(block):
        return jnp.concatenate([quad, quad, local_ids(block, 0), local_ids(block, 1)], axis=1)

    for turn in range(ROTATIONS):
        piece = images_ref[:, turn * shift : (turn + 1) * shift].astype(jnp.float32) * factor
        piece = piece.astype(jnp.bfloat16).astype(jnp.float32)
        own_wide[turn * part_dev : (turn + 1) * part_dev, :] = piece
        group_wide[turn * group : turn * group + part_dev, :] = piece
    own_wide[own_rows : own_rows + 16, :] = jnp.zeros((16, shift), jnp.float32)
    own_wide[own_rows : own_rows + part_dev, :] = extras(1 - side)
    own_send[...] = own_wide[...].astype(jnp.bfloat16)

    pl.semaphore_wait(barrier, doms)
    swap = pltpu.make_async_remote_copy(
        src_ref=own_send,
        dst_ref=other_recv,
        send_sem=pair_send_sem.at[0],
        recv_sem=pair_recv_sem.at[0],
        device_id={"cls": 1 - side},
        device_id_type=MESH,
    )
    swap.start()

    load.wait()
    energy = jnp.zeros((class_block, LANES), jnp.float32)
    for start in range(0, features, LANES):
        part = held[:, start : start + LANES].astype(jnp.float32)
        energy = energy + part * part

    swap.wait()
    other_wide[...] = other_recv[...].astype(jnp.float32)
    for turn in range(ROTATIONS):
        group_wide[turn * group + part_dev : (turn + 1) * group, :] = other_wide[
            turn * part_dev : (turn + 1) * part_dev, :
        ]
    info = jnp.concatenate([extras(side), other_wide[own_rows : own_rows + part_dev, :]], axis=0)
    quad_group = info[:, :LANES]
    first_id = info[:, 2 * cycles : 2 * cycles + 1]
    second_id = info[:, 3 * cycles : 3 * cycles + 1]

    ids_send[...] = jnp.broadcast_to(
        jnp.concatenate([first_id, second_id], axis=0), (pairs, LANES)
    ).astype(jnp.bfloat16)
    mine = pl.ds(pl.multiple_of(me * pairs, pairs), pairs)
    ids_recv[mine, :] = ids_send[...]
    id_copies = []
    for step, peer in enumerate(peers):
        copy = pltpu.make_async_remote_copy(
            src_ref=ids_send,
            dst_ref=ids_recv.at[mine, :],
            send_sem=ids_send_sem.at[step],
            recv_sem=ids_recv_sem.at[step],
            device_id={"dom": peer},
            device_id_type=MESH,
        )
        copy.start()
        id_copies.append(copy)

    even = group_wide[...].astype(jnp.bfloat16)
    odd = jnp.concatenate([group_wide[group:, :], group_wide[:group, :]], axis=0).astype(
        jnp.bfloat16
    )
    twin_even[:rows, :] = even
    twin_even[rows:, :] = even
    twin_odd[:rows, :] = odd
    twin_odd[rows:, :] = odd
    for turn in range(ROTATIONS):
        window = twin_odd if turn % 2 else twin_even
        begin = (turn - turn % 2) * group
        framed[:, turn * shift : (turn + 1) * shift] = window[begin : begin + rows, :]

    contract_last = (((1,), (1,)), ((), ()))
    cross = lax.dot_general(
        held[...], framed[...], contract_last, preferred_element_type=jnp.float32
    )
    norm = lax.dot_general(
        energy,
        jnp.concatenate([quad_group] * ROTATIONS, axis=0),
        contract_last,
        precision=lax.Precision.HIGHEST,
        preferred_element_type=jnp.float32,
    )
    logits = cross - 0.5 * norm

    lane = lax.broadcasted_iota(jnp.int32, (group, rows), 1)
    own_lane = (lane & (group - 1)) == lax.broadcasted_iota(jnp.int32, (group, rows), 0)
    class_row = lax.broadcasted_iota(jnp.int32, (class_block, rows), 0).astype(jnp.float32)

    def pick(ids):
        wanted = jnp.sum(jnp.where(own_lane, ids, 0.0), axis=0, keepdims=True)
        value = jnp.sum(jnp.where(class_row == wanted, logits, 0.0), axis=0, keepdims=True)
        live = own_lane & (ids >= 0.0)
        return live, jnp.broadcast_to(value, (group, rows))

    live_a, value_a = pick(first_id)
    live_b, value_b = pick(second_id)
    masked_a = jnp.where(live_a, value_a, NEGATIVE)
    masked_b = jnp.where(live_b, value_b, NEGATIVE)
    peak = jnp.max(jnp.maximum(masked_a, masked_b), axis=1, keepdims=True)
    total = jnp.sum(
        jnp.where(live_a, jnp.exp(masked_a - peak), 0.0)
        + jnp.where(live_b, jnp.exp(masked_b - peak), 0.0),
        axis=1,
        keepdims=True,
    )
    half = lax.broadcasted_iota(jnp.int32, (group, LANES), 1) < LANES // 2
    part_send[...] = jnp.where(half, peak, total)
    share_part = pltpu.make_async_remote_copy(
        src_ref=part_send,
        dst_ref=part_recv,
        send_sem=pair_send_sem.at[1],
        recv_sem=pair_recv_sem.at[1],
        device_id={"cls": 1 - side},
        device_id_type=MESH,
    )
    share_part.start()
    share_part.wait()
    theirs = part_recv[...]
    theirs = jnp.concatenate([theirs[part_dev:, :], theirs[:part_dev, :]], axis=0)
    their_peak = theirs[:, :1]
    their_total = theirs[:, LANES // 2 : LANES // 2 + 1]
    top = jnp.maximum(peak, their_peak)
    both = total * jnp.exp(peak - top) + their_total * jnp.exp(their_peak - top)
    evidence = top + jnp.log(both)
    corner = lax.broadcasted_iota(jnp.int32, (group, LANES), 1) == lax.broadcasted_iota(
        jnp.int32, (group, LANES), 0
    )
    evidence_row = jnp.sum(jnp.where(corner, evidence, 0.0), axis=0, keepdims=True)
    evidence_ref[...] = evidence_row[:, :part_dev]

    posterior = jnp.concatenate(
        [
            jnp.where(live_a, jnp.exp(masked_a - evidence), 0.0),
            jnp.where(live_b, jnp.exp(masked_b - evidence), 0.0),
        ],
        axis=0,
    ).astype(jnp.bfloat16)
    weight = jnp.sum(posterior.astype(jnp.float32), axis=1, keepdims=True)
    filters = (weight * jnp.concatenate([quad_group, quad_group], axis=0)).astype(jnp.bfloat16)
    terms = jnp.dot(posterior, framed[...], preferred_element_type=jnp.float32).astype(
        jnp.bfloat16
    )
    low_lanes = lax.broadcasted_iota(jnp.int32, (pairs, LANES), 1) < cycles
    for target in range(doms):
        begin = target * share // LANES * LANES
        here = slice(target * pairs, (target + 1) * pairs)
        if target * share == begin:
            edge = begin + wide - LANES
            stage[here, : wide - LANES] = terms[:, begin:edge]
            stage[here, wide - LANES :] = jnp.where(low_lanes, terms[:, edge : edge + LANES], filters)
        else:
            stage[here, :LANES] = jnp.where(low_lanes, filters, terms[:, begin : begin + LANES])
            stage[here, LANES:] = terms[:, begin + LANES : begin + wide]
    copies = []
    for step, peer in enumerate(peers):
        copy = pltpu.make_async_remote_copy(
            src_ref=stage.at[pl.ds(pl.multiple_of(peer * pairs, pairs), pairs), :],
            dst_ref=arrived.at[mine, :],
            send_sem=data_send_sem.at[step],
            recv_sem=data_recv_sem.at[step],
            device_id={"dom": peer},
            device_id_type=MESH,
        )
        copy.start()
        copies.append(copy)
    arrived[mine, :] = stage[mine, :]

    for copy in id_copies:
        copy.wait()
    ids = jnp.broadcast_to(
        ids_recv[...].astype(jnp.float32)[:, :1], (doms * pairs, class_block)
    )
    column = lax.broadcasted_iota(jnp.int32, (doms * pairs, class_block), 1).astype(jnp.float32)
    chosen = jnp.where(ids == column, 1.0, 0.0).astype(jnp.bfloat16)
    for copy in copies:
        copy.wait()
    contract_first = (((0,), (0,)), ((), ()))
    late = lax.rem(me, 2) == 1
    everything = arrived[...]
    sums = lax.dot_general(
        everything, chosen, contract_first, preferred_element_type=jnp.float32
    )
    sums_ref[...] = jnp.where(late, sums[wide - share :, :], sums[:share, :])
    filter_part = jnp.where(late, everything[:, :LANES], everything[:, wide - LANES :])
    filter_sums = lax.dot_general(
        chosen, filter_part, contract_first, preferred_element_type=jnp.float32
    )
    weight_ref[...] = jnp.where(late, filter_sums[:, :cycles], filter_sums[:, cycles:])


def paired_shards(images, ctf, inv_noise, classes, candidates):
    doms = lax.axis_size("dom")
    part_dev, features = images.shape
    cycles = ctf.shape[1]
    class_block = classes.shape[0]
    shift = features // ROTATIONS
    group = 2 * part_dev
    rows = ROTATIONS * group
    pairs = TOP_CAND * group
    share = features // doms
    wide = share + cycles
    own_rows = ROTATIONS * part_dev + 16
    f32, bf16 = jnp.float32, jnp.bfloat16
    vmem = pl.BlockSpec(memory_space=pltpu.VMEM)
    sums, weight, evidence = pl.pallas_call(
        functools.partial(estep_kernel, doms),
        out_shape=(
            jax.ShapeDtypeStruct((share, class_block), f32),
            jax.ShapeDtypeStruct((class_block, cycles), f32),
            jax.ShapeDtypeStruct((1, part_dev), f32),
        ),
        in_specs=[vmem] * 4 + [pl.BlockSpec(memory_space=pl.ANY)],
        out_specs=(vmem, vmem, vmem),
        scratch_shapes=[
            pltpu.VMEM((class_block, features), bf16),
            pltpu.VMEM((own_rows, shift), f32),
            pltpu.VMEM((own_rows, shift), bf16),
            pltpu.VMEM((own_rows, shift), bf16),
            pltpu.VMEM((own_rows, shift), f32),
            pltpu.VMEM((rows, shift), f32),
            pltpu.VMEM((2 * rows, shift), bf16),
            pltpu.VMEM((2 * rows, shift), bf16),
            pltpu.VMEM((rows, features), bf16),
            pltpu.VMEM((group, LANES), f32),
            pltpu.VMEM((group, LANES), f32),
            pltpu.VMEM((pairs, LANES), bf16),
            pltpu.VMEM((doms * pairs, LANES), bf16),
            pltpu.VMEM((doms * pairs, wide), bf16),
            pltpu.VMEM((doms * pairs, wide), bf16),
            pltpu.SemaphoreType.DMA,
            pltpu.SemaphoreType.DMA((2,)),
            pltpu.SemaphoreType.DMA((2,)),
            pltpu.SemaphoreType.DMA((doms - 1,)),
            pltpu.SemaphoreType.DMA((doms - 1,)),
            pltpu.SemaphoreType.DMA((doms - 1,)),
            pltpu.SemaphoreType.DMA((doms - 1,)),
        ],
        compiler_params=pltpu.CompilerParams(
            collective_id=0, has_side_effects=True, vmem_limit_bytes=40 * 1024 * 1024
        ),
    )(images, ctf, inv_noise[None, :], candidates, classes)
    return sums, weight, evidence.reshape(part_dev)


def pick_plan(images, ctf, inv_noise, classes, candidates):
    doms = lax.axis_size("dom")
    part_dev, features = images.shape
    cycles = ctf.shape[1]
    fits = (
        lax.axis_size("cls") == 2
        and part_dev == 4
        and 2 * cycles == LANES
        and features == ROTATIONS * 2 * LANES
        and doms % 2 == 0
        and (features // doms) % LANES == cycles
        and classes.shape[0] <= 256
    )
    plan = paired_shards if fits else shards
    return plan(images, ctf, inv_noise, classes, candidates)


def solution(mesh):
    in_specs = (
        P(("dom", "cls"), None),
        P(("dom", "cls"), None),
        P(),
        P("cls", None),
        P(("dom", "cls"), None),
    )
    out_specs = (P("dom", "cls"), P("cls", None), P(("dom", "cls")))
    return jax.shard_map(
        pick_plan, mesh=mesh, in_specs=in_specs, out_specs=out_specs, check_vma=False
    )
```

```python
import functools
import math

import jax
import jax.numpy as jnp
from jax import lax
from jax.experimental import pallas as pl
from jax.experimental.pallas import tpu as pltpu
from jax.sharding import PartitionSpec as P

ANGLES = 72
ROTATIONS = 36
TOP_CAND = 2


NEGATIVE = -1e30


def combined_all(value, axis, join):
    pieces = jax.tree.map(lambda part: lax.all_gather(part, axis), value)
    head = jax.tree.map(lambda part: part[0], pieces)
    tail = jax.tree.map(lambda part: part[1:], pieces)
    subtotal, _ = lax.scan(lambda subtotal, section: (join(subtotal, section), None), head, tail)
    return subtotal


def combine_totals(earlier, later):
    highest = jnp.maximum(earlier[0], later[0])
    return (
        highest,
        earlier[1] * jnp.exp(earlier[0] - highest) + later[1] * jnp.exp(later[0] - highest),
    )


def shards(images, ctf, inv_noise, classes, candidates):
    cls_count = lax.axis_size("cls")
    my_index = lax.axis_index("cls")
    part_dev = images.shape[0]
    class_block = classes.shape[0]
    features = images.shape[1]
    cycles = ctf.shape[1]
    capacity = min(5 * part_dev * TOP_CAND // (2 * cls_count), part_dev)
    group_size = cls_count * part_dev
    shift = features // ANGLES * (ANGLES // ROTATIONS)
    turn_ids = jnp.arange(ROTATIONS, dtype=jnp.int32)
    ctf_noise = ctf * inv_noise[None, :]
    weighted = (images.astype(jnp.float32) * jnp.tile(ctf_noise, (1, features // cycles))).astype(
        jnp.bfloat16
    )
    quadratic = (ctf * ctf * inv_noise[None, :]).astype(jnp.bfloat16)
    everyone = lax.all_gather(candidates, "cls", axis=0, tiled=True)
    block_ids = jnp.arange(class_block, dtype=jnp.int32) + my_index * class_block
    cand_mask = jnp.any(everyone[:, :, None] == block_ids[None, None, :], axis=1).astype(
        jnp.float32
    )
    owner_ids = jnp.arange(cls_count, dtype=jnp.int32)
    routed = jnp.any(
        (everyone // class_block)[:, :, None] == owner_ids[None, None, :], axis=1
    ).astype(jnp.int32)
    by_source = routed.reshape(cls_count, part_dev, cls_count)
    slot_of = jnp.cumsum(by_source, axis=1) - by_source
    slot_ids = jnp.arange(capacity, dtype=jnp.int32)
    mine_routed = lax.dynamic_index_in_dim(by_source, my_index, 0, keepdims=False)
    mine_slot = lax.dynamic_index_in_dim(slot_of, my_index, 0, keepdims=False)
    packing = (mine_routed.T[:, None, :] == 1) & (
        mine_slot.T[:, None, :] == slot_ids[None, :, None]
    )
    packing = packing.reshape(cls_count * capacity, part_dev).astype(jnp.bfloat16)
    send_data = jnp.dot(packing, weighted, preferred_element_type=jnp.float32).astype(jnp.bfloat16)
    send_quad = jnp.dot(packing, quadratic, preferred_element_type=jnp.float32).astype(jnp.bfloat16)
    row_data, row_quad = (
        lax.all_to_all(send_data, "cls", split_axis=0, concat_axis=0, tiled=True),
        lax.all_to_all(send_quad, "cls", split_axis=0, concat_axis=0, tiled=True),
    )
    into_mine = lax.dynamic_index_in_dim(by_source, my_index, 2, keepdims=False)
    slot_mine = lax.dynamic_index_in_dim(slot_of, my_index, 2, keepdims=False)
    selected = (into_mine[:, None, :] == 1) & (slot_mine[:, None, :] == slot_ids[None, :, None])
    diagonal = jnp.eye(cls_count, dtype=jnp.float32)
    unpack = (selected.astype(jnp.float32)[:, :, None, :] * diagonal[:, None, :, None]).reshape(
        cls_count * capacity, group_size
    )
    row_mask = jnp.dot(unpack, cand_mask, precision=lax.Precision.HIGHEST)
    row_count = row_data.shape[0]
    energy = jnp.sum(
        jnp.square(classes.astype(jnp.float32)).reshape(class_block, features // cycles, cycles),
        axis=1,
    )
    quad_wide = row_quad.astype(jnp.float32)
    norm_term = jnp.dot(quad_wide, energy.T, precision=lax.Precision.HIGHEST)
    twin_classes = jnp.concatenate([classes, classes], axis=1)
    feat_block = math.gcd(features, 1152)

    def add_block(block_index, running):
        offset = block_index * feat_block
        rotated = jax.vmap(
            lambda rotation: lax.dynamic_slice_in_dim(
                twin_classes, offset - rotation * shift + features, feat_block, 1
            )
        )(turn_ids)
        section = lax.dynamic_slice_in_dim(row_data, offset, feat_block, 1)
        return running + lax.dot_general(
            section, rotated, (((1,), (2,)), ((), ())), preferred_element_type=jnp.float32
        )

    cross = lax.fori_loop(
        0,
        features // feat_block,
        add_block,
        jnp.zeros((row_count, ROTATIONS, class_block), jnp.float32),
    )
    logits = cross - 0.5 * norm_term[:, None, :]
    live = jnp.broadcast_to(row_mask[:, None, :] > 0.5, logits.shape)
    masked = jnp.where(live, logits, NEGATIVE)
    peak = jnp.max(masked, axis=(1, 2))
    part_total = jnp.sum(jnp.where(live, jnp.exp(masked - peak[:, None, None]), 0.0), axis=(1, 2))
    group_peak = jnp.max(jnp.where(unpack > 0.5, peak[:, None], NEGATIVE), axis=0)
    group_total = jnp.sum(unpack * part_total[:, None], axis=0)
    top_all, total_all = combined_all((group_peak, group_total), "cls", combine_totals)
    group_evidence = top_all + jnp.log(total_all)
    own_evidence = lax.dynamic_slice_in_dim(group_evidence, my_index * part_dev, part_dev, 0)
    row_evidence = jnp.dot(unpack, group_evidence, precision=lax.Precision.HIGHEST)
    posterior = jnp.where(live, jnp.exp(logits - row_evidence[:, None, None]), 0.0).astype(
        jnp.bfloat16
    )
    weight_total = jnp.sum(posterior.astype(jnp.float32), axis=1)
    ctf_part = jnp.dot(weight_total.T, quad_wide, precision=lax.Precision.HIGHEST)
    weight_sums = lax.psum(ctf_part, "dom")
    twin_rows = jnp.concatenate([row_data, row_data], axis=1)

    def add_sums(block_index, running):
        offset = block_index * feat_block
        stacked = jax.vmap(
            lambda rotation: lax.dynamic_slice_in_dim(
                twin_rows, offset + rotation * shift, feat_block, 1
            )
        )(turn_ids)
        block_sum = lax.dot_general(
            posterior, stacked, (((0, 1), (1, 0)), ((), ())), preferred_element_type=jnp.float32
        )
        return lax.dynamic_update_slice_in_dim(running, block_sum, offset, 1)

    summed = lax.fori_loop(
        0, features // feat_block, add_sums, jnp.zeros((class_block, features), jnp.float32)
    )
    full_term = summed.T
    class_sums = lax.psum_scatter(full_term, "dom", scatter_dimension=0, tiled=True)
    return (class_sums, weight_sums, own_evidence)


MESH = pl.DeviceIdType.MESH
LANES = 128


def estep_kernel(
    doms,
    images_ref,
    ctf_ref,
    noise_ref,
    cand_ref,
    classes_ref,
    arrived,
    chosen_ref,
    evidence_ref,
    held,
    images_vmem,
    ctf_vmem,
    noise_vmem,
    cand_vmem,
    own_wide,
    own_send,
    other_recv,
    other_wide,
    group_wide,
    twin_even,
    twin_odd,
    framed,
    part_send,
    part_recv,
    ids_send,
    ids_recv,
    stage,
    load_sem,
    pair_send_sem,
    pair_recv_sem,
    ids_send_sem,
    ids_recv_sem,
    data_send_sem,
    data_recv_sem,
):
    me = lax.axis_index("dom")
    side = lax.axis_index("cls")
    part_dev, features = images_ref.shape
    cycles = ctf_ref.shape[1]
    class_block = held.shape[0]
    shift = framed.shape[1] // ROTATIONS
    group = 2 * part_dev
    rows = ROTATIONS * group
    pairs = TOP_CAND * group
    own_rows = ROTATIONS * part_dev
    share = features // doms
    wide = stage.shape[1]
    peers = [lax.rem(me + step, doms) for step in range(1, doms)]

    loads = [
        pltpu.make_async_copy(source, target, load_sem.at[place])
        for place, (source, target) in enumerate(
            [
                (cand_ref, cand_vmem),
                (noise_ref, noise_vmem),
                (ctf_ref, ctf_vmem),
                (images_ref, images_vmem),
                (classes_ref, held),
            ]
        )
    ]
    for load in loads:
        load.start()
    barrier = pltpu.get_barrier_semaphore()
    pl.semaphore_signal(barrier, inc=1, device_id={"cls": 1 - side}, device_id_type=MESH)
    for peer in peers:
        pl.semaphore_signal(barrier, inc=1, device_id={"dom": peer}, device_id_type=MESH)

    for load in loads[:4]:
        load.wait()
    ctf = ctf_vmem[...]
    noise = noise_vmem[...]
    factor = jnp.concatenate([ctf * noise] * (shift // cycles), axis=1)
    quad = (ctf * ctf * noise).astype(jnp.bfloat16).astype(jnp.float32)
    cand = cand_vmem[...].astype(jnp.float32)
    square = (part_dev, part_dev)
    same = lax.broadcasted_iota(jnp.int32, square, 0) == lax.broadcasted_iota(jnp.int32, square, 1)

    def local_ids(block, column):
        ids = jnp.broadcast_to(cand[column : column + 1, :], square)
        ids = jnp.sum(jnp.where(same, ids, 0.0), axis=1, keepdims=True)
        local = ids - (block * class_block).astype(jnp.float32)
        inside = (local >= 0.0) & (local < class_block)
        return jnp.broadcast_to(jnp.where(inside, local, -1.0), (part_dev, cycles))

    def extras(block):
        return jnp.concatenate([quad, quad, local_ids(block, 0), local_ids(block, 1)], axis=1)

    for turn in range(ROTATIONS):
        piece = images_vmem[:, turn * shift : (turn + 1) * shift].astype(jnp.float32) * factor
        piece = piece.astype(jnp.bfloat16).astype(jnp.float32)
        own_wide[turn * part_dev : (turn + 1) * part_dev, :] = piece
        group_wide[turn * group : turn * group + part_dev, :] = piece
    own_wide[own_rows : own_rows + 16, :] = jnp.zeros((16, shift), jnp.float32)
    own_wide[own_rows : own_rows + part_dev, :] = extras(1 - side)
    own_send[...] = own_wide[...].astype(jnp.bfloat16)

    pl.semaphore_wait(barrier, doms)
    swap = pltpu.make_async_remote_copy(
        src_ref=own_send,
        dst_ref=other_recv,
        send_sem=pair_send_sem.at[0],
        recv_sem=pair_recv_sem.at[0],
        device_id={"cls": 1 - side},
        device_id_type=MESH,
    )
    swap.start()

    loads[4].wait()
    energy = jnp.zeros((class_block, LANES), jnp.float32)
    for start in range(0, features, LANES):
        part = held[:, start : start + LANES].astype(jnp.float32)
        energy = energy + part * part

    swap.wait()
    other_wide[...] = other_recv[...].astype(jnp.float32)
    for turn in range(ROTATIONS):
        group_wide[turn * group + part_dev : (turn + 1) * group, :] = other_wide[
            turn * part_dev : (turn + 1) * part_dev, :
        ]
    info = jnp.concatenate([extras(side), other_wide[own_rows : own_rows + part_dev, :]], axis=0)
    quad_group = info[:, :LANES]
    first_id = info[:, 2 * cycles : 2 * cycles + 1]
    second_id = info[:, 3 * cycles : 3 * cycles + 1]

    ids_send[...] = jnp.broadcast_to(
        jnp.concatenate([first_id, second_id], axis=0), (pairs, LANES)
    ).astype(jnp.bfloat16)
    mine = pl.ds(pl.multiple_of(me * pairs, pairs), pairs)
    ids_recv[mine, :] = ids_send[...]
    id_copies = []
    for step, peer in enumerate(peers):
        copy = pltpu.make_async_remote_copy(
            src_ref=ids_send,
            dst_ref=ids_recv.at[mine, :],
            send_sem=ids_send_sem.at[step],
            recv_sem=ids_recv_sem.at[step],
            device_id={"dom": peer},
            device_id_type=MESH,
        )
        copy.start()
        id_copies.append(copy)

    even = group_wide[...].astype(jnp.bfloat16)
    odd = jnp.concatenate([group_wide[group:, :], group_wide[:group, :]], axis=0).astype(
        jnp.bfloat16
    )
    twin_even[:rows, :] = even
    twin_even[rows:, :] = even
    twin_odd[:rows, :] = odd
    twin_odd[rows:, :] = odd
    for turn in range(ROTATIONS):
        window = twin_odd if turn % 2 else twin_even
        begin = (turn - turn % 2) * group
        framed[:, turn * shift : (turn + 1) * shift] = window[begin : begin + rows, :]

    contract_last = (((1,), (1,)), ((), ()))
    cross = lax.dot_general(
        held[...], framed[...], contract_last, preferred_element_type=jnp.float32
    )
    norm = lax.dot_general(
        energy,
        jnp.concatenate([quad_group] * ROTATIONS, axis=0),
        contract_last,
        precision=lax.Precision.HIGHEST,
        preferred_element_type=jnp.float32,
    )
    logits = cross - 0.5 * norm

    lane = lax.broadcasted_iota(jnp.int32, (group, rows), 1)
    own_lane = (lane & (group - 1)) == lax.broadcasted_iota(jnp.int32, (group, rows), 0)
    class_row = lax.broadcasted_iota(jnp.int32, (class_block, rows), 0).astype(jnp.float32)

    def pick(ids):
        wanted = jnp.sum(jnp.where(own_lane, ids, 0.0), axis=0, keepdims=True)
        value = jnp.sum(jnp.where(class_row == wanted, logits, 0.0), axis=0, keepdims=True)
        live = own_lane & (ids >= 0.0)
        return live, jnp.broadcast_to(value, (group, rows))

    live_a, value_a = pick(first_id)
    live_b, value_b = pick(second_id)
    masked_a = jnp.where(live_a, value_a, NEGATIVE)
    masked_b = jnp.where(live_b, value_b, NEGATIVE)
    peak = jnp.max(jnp.maximum(masked_a, masked_b), axis=1, keepdims=True)
    total = jnp.sum(
        jnp.where(live_a, jnp.exp(masked_a - peak), 0.0)
        + jnp.where(live_b, jnp.exp(masked_b - peak), 0.0),
        axis=1,
        keepdims=True,
    )
    half = lax.broadcasted_iota(jnp.int32, (group, LANES), 1) < LANES // 2
    part_send[...] = jnp.where(half, peak, total)
    share_part = pltpu.make_async_remote_copy(
        src_ref=part_send,
        dst_ref=part_recv,
        send_sem=pair_send_sem.at[1],
        recv_sem=pair_recv_sem.at[1],
        device_id={"cls": 1 - side},
        device_id_type=MESH,
    )
    share_part.start()
    share_part.wait()
    theirs = part_recv[...]
    theirs = jnp.concatenate([theirs[part_dev:, :], theirs[:part_dev, :]], axis=0)
    their_peak = theirs[:, :1]
    their_total = theirs[:, LANES // 2 : LANES // 2 + 1]
    top = jnp.maximum(peak, their_peak)
    both = total * jnp.exp(peak - top) + their_total * jnp.exp(their_peak - top)
    evidence = top + jnp.log(both)
    corner = lax.broadcasted_iota(jnp.int32, (group, LANES), 1) == lax.broadcasted_iota(
        jnp.int32, (group, LANES), 0
    )
    evidence_row = jnp.sum(jnp.where(corner, evidence, 0.0), axis=0, keepdims=True)
    evidence_ref[...] = evidence_row[:, :part_dev]

    posterior = jnp.concatenate(
        [
            jnp.where(live_a, jnp.exp(masked_a - evidence), 0.0),
            jnp.where(live_b, jnp.exp(masked_b - evidence), 0.0),
        ],
        axis=0,
    ).astype(jnp.bfloat16)
    weight = jnp.sum(posterior.astype(jnp.float32), axis=1, keepdims=True)
    filters = (weight * jnp.concatenate([quad_group, quad_group], axis=0)).astype(jnp.bfloat16)
    terms = jnp.dot(posterior, framed[...], preferred_element_type=jnp.float32).astype(
        jnp.bfloat16
    )
    for target in range(doms):
        here = slice(target * pairs, (target + 1) * pairs)
        stage[here, :] = jnp.concatenate(
            [terms[:, target * share : (target + 1) * share], filters[:, :cycles]], axis=1
        )
    copies = []
    for step, peer in enumerate(peers):
        copy = pltpu.make_async_remote_copy(
            src_ref=stage.at[pl.ds(pl.multiple_of(peer * pairs, pairs), pairs), :],
            dst_ref=arrived.at[mine, :],
            send_sem=data_send_sem.at[step],
            recv_sem=data_recv_sem.at[step],
            device_id={"dom": peer},
            device_id_type=MESH,
        )
        copy.start()
        copies.append(copy)
    arrived[mine, :] = stage[mine, :]

    for copy in id_copies:
        copy.wait()
    ids = jnp.broadcast_to(
        ids_recv[...].astype(jnp.float32)[:, :1], (doms * pairs, class_block)
    )
    column = lax.broadcasted_iota(jnp.int32, (doms * pairs, class_block), 1).astype(jnp.float32)
    chosen_ref[...] = jnp.where(ids == column, 1.0, 0.0).astype(jnp.bfloat16)
    for copy in copies:
        copy.wait()


def sums_kernel(arrived, chosen, evidence_in, sums_ref, weight_ref, evidence_ref):
    share = sums_ref.shape[1]
    cycles = weight_ref.shape[0]
    contract_first = (((0,), (0,)), ((), ()))
    evidence_ref[...] = evidence_in[...]
    sums = lax.dot_general(
        chosen[...], arrived[...], contract_first, preferred_element_type=jnp.float32
    )
    sums_ref[...] = sums[:, :share]
    filter_sums = lax.dot_general(
        arrived[:, share - cycles :],
        chosen[...],
        contract_first,
        preferred_element_type=jnp.float32,
    )
    weight_ref[...] = filter_sums[cycles:, :]


def paired_shards(images, ctf, inv_noise, classes, candidates):
    doms = lax.axis_size("dom")
    part_dev, features = images.shape
    cycles = ctf.shape[1]
    class_block = classes.shape[0]
    shift = features // ROTATIONS
    group = 2 * part_dev
    rows = ROTATIONS * group
    pairs = TOP_CAND * group
    share = features // doms
    wide = share + cycles
    own_rows = ROTATIONS * part_dev + 16
    f32, bf16 = jnp.float32, jnp.bfloat16
    vmem = pl.BlockSpec(memory_space=pltpu.VMEM)
    arrived, chosen, evidence = pl.pallas_call(
        functools.partial(estep_kernel, doms),
        out_shape=(
            jax.ShapeDtypeStruct((doms * pairs, wide), bf16),
            jax.ShapeDtypeStruct((doms * pairs, class_block), bf16),
            jax.ShapeDtypeStruct((1, part_dev), f32),
        ),
        in_specs=[pl.BlockSpec(memory_space=pltpu.HBM)] * 5,
        out_specs=(vmem, vmem, vmem),
        scratch_shapes=[
            pltpu.VMEM((class_block, features), bf16),
            pltpu.VMEM((part_dev, features), bf16),
            pltpu.VMEM((part_dev, cycles), f32),
            pltpu.VMEM((1, cycles), f32),
            pltpu.VMEM((TOP_CAND, part_dev), jnp.int32),
            pltpu.VMEM((own_rows, shift), f32),
            pltpu.VMEM((own_rows, shift), bf16),
            pltpu.VMEM((own_rows, shift), bf16),
            pltpu.VMEM((own_rows, shift), f32),
            pltpu.VMEM((rows, shift), f32),
            pltpu.VMEM((2 * rows, shift), bf16),
            pltpu.VMEM((2 * rows, shift), bf16),
            pltpu.VMEM((rows, features), bf16),
            pltpu.VMEM((group, LANES), f32),
            pltpu.VMEM((group, LANES), f32),
            pltpu.VMEM((pairs, LANES), bf16),
            pltpu.VMEM((doms * pairs, LANES), bf16),
            pltpu.VMEM((doms * pairs, wide), bf16),
            pltpu.SemaphoreType.DMA((5,)),
            pltpu.SemaphoreType.DMA((2,)),
            pltpu.SemaphoreType.DMA((2,)),
            pltpu.SemaphoreType.DMA((doms - 1,)),
            pltpu.SemaphoreType.DMA((doms - 1,)),
            pltpu.SemaphoreType.DMA((doms - 1,)),
            pltpu.SemaphoreType.DMA((doms - 1,)),
        ],
        compiler_params=pltpu.CompilerParams(
            collective_id=0, has_side_effects=True, vmem_limit_bytes=63 * 1024 * 1024
        ),
    )(images, ctf, inv_noise[None, :], candidates.T, classes)
    sums, weight, evidence = pl.pallas_call(
        sums_kernel,
        out_shape=(
            jax.ShapeDtypeStruct((class_block, share), f32),
            jax.ShapeDtypeStruct((cycles, class_block), f32),
            jax.ShapeDtypeStruct((1, part_dev), f32),
        ),
        in_specs=[vmem] * 3,
        out_specs=(vmem, vmem, vmem),
        compiler_params=pltpu.CompilerParams(vmem_limit_bytes=63 * 1024 * 1024),
    )(arrived, chosen, evidence)
    return sums.T, weight.T, evidence.reshape(part_dev)


def pick_plan(images, ctf, inv_noise, classes, candidates):
    doms = lax.axis_size("dom")
    part_dev, features = images.shape
    cycles = ctf.shape[1]
    fits = (
        lax.axis_size("cls") == 2
        and part_dev == 4
        and 2 * cycles == LANES
        and features == ROTATIONS * 2 * LANES
        and doms % 2 == 0
        and (features // doms) % LANES == cycles
        and classes.shape[0] <= 256
    )
    plan = paired_shards if fits else shards
    return plan(images, ctf, inv_noise, classes, candidates)


def solution(mesh):
    in_specs = (
        P(("dom", "cls"), None),
        P(("dom", "cls"), None),
        P(),
        P("cls", None),
        P(("dom", "cls"), None),
    )
    out_specs = (P("dom", "cls"), P("cls", None), P(("dom", "cls")))
    return jax.shard_map(
        pick_plan, mesh=mesh, in_specs=in_specs, out_specs=out_specs, check_vma=False
    )
```

```python
import functools
import math

import jax
import jax.numpy as jnp
from jax import lax
from jax.experimental import pallas as pl
from jax.experimental.pallas import tpu as pltpu
from jax.sharding import PartitionSpec as P

ANGLES = 72
ROTATIONS = 36
TOP_CAND = 2


NEGATIVE = -1e30


def combined_all(value, axis, join):
    pieces = jax.tree.map(lambda part: lax.all_gather(part, axis), value)
    head = jax.tree.map(lambda part: part[0], pieces)
    tail = jax.tree.map(lambda part: part[1:], pieces)
    subtotal, _ = lax.scan(lambda subtotal, section: (join(subtotal, section), None), head, tail)
    return subtotal


def combine_totals(earlier, later):
    highest = jnp.maximum(earlier[0], later[0])
    return (
        highest,
        earlier[1] * jnp.exp(earlier[0] - highest) + later[1] * jnp.exp(later[0] - highest),
    )


def shards(images, ctf, inv_noise, classes, candidates):
    cls_count = lax.axis_size("cls")
    my_index = lax.axis_index("cls")
    part_dev = images.shape[0]
    class_block = classes.shape[0]
    features = images.shape[1]
    cycles = ctf.shape[1]
    capacity = min(5 * part_dev * TOP_CAND // (2 * cls_count), part_dev)
    group_size = cls_count * part_dev
    shift = features // ANGLES * (ANGLES // ROTATIONS)
    turn_ids = jnp.arange(ROTATIONS, dtype=jnp.int32)
    ctf_noise = ctf * inv_noise[None, :]
    weighted = (images.astype(jnp.float32) * jnp.tile(ctf_noise, (1, features // cycles))).astype(
        jnp.bfloat16
    )
    quadratic = (ctf * ctf * inv_noise[None, :]).astype(jnp.bfloat16)
    everyone = lax.all_gather(candidates, "cls", axis=0, tiled=True)
    block_ids = jnp.arange(class_block, dtype=jnp.int32) + my_index * class_block
    cand_mask = jnp.any(everyone[:, :, None] == block_ids[None, None, :], axis=1).astype(
        jnp.float32
    )
    owner_ids = jnp.arange(cls_count, dtype=jnp.int32)
    routed = jnp.any(
        (everyone // class_block)[:, :, None] == owner_ids[None, None, :], axis=1
    ).astype(jnp.int32)
    by_source = routed.reshape(cls_count, part_dev, cls_count)
    slot_of = jnp.cumsum(by_source, axis=1) - by_source
    slot_ids = jnp.arange(capacity, dtype=jnp.int32)
    mine_routed = lax.dynamic_index_in_dim(by_source, my_index, 0, keepdims=False)
    mine_slot = lax.dynamic_index_in_dim(slot_of, my_index, 0, keepdims=False)
    packing = (mine_routed.T[:, None, :] == 1) & (
        mine_slot.T[:, None, :] == slot_ids[None, :, None]
    )
    packing = packing.reshape(cls_count * capacity, part_dev).astype(jnp.bfloat16)
    send_data = jnp.dot(packing, weighted, preferred_element_type=jnp.float32).astype(jnp.bfloat16)
    send_quad = jnp.dot(packing, quadratic, preferred_element_type=jnp.float32).astype(jnp.bfloat16)
    row_data, row_quad = (
        lax.all_to_all(send_data, "cls", split_axis=0, concat_axis=0, tiled=True),
        lax.all_to_all(send_quad, "cls", split_axis=0, concat_axis=0, tiled=True),
    )
    into_mine = lax.dynamic_index_in_dim(by_source, my_index, 2, keepdims=False)
    slot_mine = lax.dynamic_index_in_dim(slot_of, my_index, 2, keepdims=False)
    selected = (into_mine[:, None, :] == 1) & (slot_mine[:, None, :] == slot_ids[None, :, None])
    diagonal = jnp.eye(cls_count, dtype=jnp.float32)
    unpack = (selected.astype(jnp.float32)[:, :, None, :] * diagonal[:, None, :, None]).reshape(
        cls_count * capacity, group_size
    )
    row_mask = jnp.dot(unpack, cand_mask, precision=lax.Precision.HIGHEST)
    row_count = row_data.shape[0]
    energy = jnp.sum(
        jnp.square(classes.astype(jnp.float32)).reshape(class_block, features // cycles, cycles),
        axis=1,
    )
    quad_wide = row_quad.astype(jnp.float32)
    norm_term = jnp.dot(quad_wide, energy.T, precision=lax.Precision.HIGHEST)
    twin_classes = jnp.concatenate([classes, classes], axis=1)
    feat_block = math.gcd(features, 1152)

    def add_block(block_index, running):
        offset = block_index * feat_block
        rotated = jax.vmap(
            lambda rotation: lax.dynamic_slice_in_dim(
                twin_classes, offset - rotation * shift + features, feat_block, 1
            )
        )(turn_ids)
        section = lax.dynamic_slice_in_dim(row_data, offset, feat_block, 1)
        return running + lax.dot_general(
            section, rotated, (((1,), (2,)), ((), ())), preferred_element_type=jnp.float32
        )

    cross = lax.fori_loop(
        0,
        features // feat_block,
        add_block,
        jnp.zeros((row_count, ROTATIONS, class_block), jnp.float32),
    )
    logits = cross - 0.5 * norm_term[:, None, :]
    live = jnp.broadcast_to(row_mask[:, None, :] > 0.5, logits.shape)
    masked = jnp.where(live, logits, NEGATIVE)
    peak = jnp.max(masked, axis=(1, 2))
    part_total = jnp.sum(jnp.where(live, jnp.exp(masked - peak[:, None, None]), 0.0), axis=(1, 2))
    group_peak = jnp.max(jnp.where(unpack > 0.5, peak[:, None], NEGATIVE), axis=0)
    group_total = jnp.sum(unpack * part_total[:, None], axis=0)
    top_all, total_all = combined_all((group_peak, group_total), "cls", combine_totals)
    group_evidence = top_all + jnp.log(total_all)
    own_evidence = lax.dynamic_slice_in_dim(group_evidence, my_index * part_dev, part_dev, 0)
    row_evidence = jnp.dot(unpack, group_evidence, precision=lax.Precision.HIGHEST)
    posterior = jnp.where(live, jnp.exp(logits - row_evidence[:, None, None]), 0.0).astype(
        jnp.bfloat16
    )
    weight_total = jnp.sum(posterior.astype(jnp.float32), axis=1)
    ctf_part = jnp.dot(weight_total.T, quad_wide, precision=lax.Precision.HIGHEST)
    weight_sums = lax.psum(ctf_part, "dom")
    twin_rows = jnp.concatenate([row_data, row_data], axis=1)

    def add_sums(block_index, running):
        offset = block_index * feat_block
        stacked = jax.vmap(
            lambda rotation: lax.dynamic_slice_in_dim(
                twin_rows, offset + rotation * shift, feat_block, 1
            )
        )(turn_ids)
        block_sum = lax.dot_general(
            posterior, stacked, (((0, 1), (1, 0)), ((), ())), preferred_element_type=jnp.float32
        )
        return lax.dynamic_update_slice_in_dim(running, block_sum, offset, 1)

    summed = lax.fori_loop(
        0, features // feat_block, add_sums, jnp.zeros((class_block, features), jnp.float32)
    )
    full_term = summed.T
    class_sums = lax.psum_scatter(full_term, "dom", scatter_dimension=0, tiled=True)
    return (class_sums, weight_sums, own_evidence)


MESH = pl.DeviceIdType.MESH
LANES = 128


def estep_kernel(
    doms,
    images_ref,
    ctf_ref,
    noise_ref,
    cand_ref,
    classes_ref,
    arrived,
    chosen_ref,
    evidence_ref,
    held,
    images_vmem,
    ctf_vmem,
    noise_vmem,
    cand_vmem,
    own_wide,
    own_send,
    other_recv,
    twins,
    own_framed,
    other_framed,
    part_send,
    part_recv,
    ids_send,
    ids_recv,
    stage,
    load_sem,
    pair_send_sem,
    pair_recv_sem,
    ids_send_sem,
    ids_recv_sem,
    data_send_sem,
    data_recv_sem,
):
    me = lax.axis_index("dom")
    side = lax.axis_index("cls")
    part_dev, features = images_ref.shape
    cycles = ctf_ref.shape[1]
    class_block = held.shape[0]
    shift = features // ROTATIONS
    group = 2 * part_dev
    pairs = TOP_CAND * group
    rows = ROTATIONS * part_dev
    share = features // doms
    wide = stage.shape[1]
    peers = [lax.rem(me + step, doms) for step in range(1, doms)]

    loads = [
        pltpu.make_async_copy(source, target, load_sem.at[place])
        for place, (source, target) in enumerate(
            [
                (cand_ref, cand_vmem),
                (noise_ref, noise_vmem),
                (ctf_ref, ctf_vmem),
                (images_ref, images_vmem),
                (classes_ref, held),
            ]
        )
    ]
    for load in loads:
        load.start()
    barrier = pltpu.get_barrier_semaphore()
    pl.semaphore_signal(barrier, inc=1, device_id={"cls": 1 - side}, device_id_type=MESH)
    for peer in peers:
        pl.semaphore_signal(barrier, inc=1, device_id={"dom": peer}, device_id_type=MESH)

    for load in loads[:4]:
        load.wait()
    ctf = ctf_vmem[...]
    noise = noise_vmem[...]
    factor = jnp.concatenate([ctf * noise] * (shift // cycles), axis=1)
    quad = (ctf * ctf * noise).astype(jnp.bfloat16).astype(jnp.float32)
    cand = cand_vmem[...].astype(jnp.float32)
    square = (part_dev, part_dev)
    same = lax.broadcasted_iota(jnp.int32, square, 0) == lax.broadcasted_iota(jnp.int32, square, 1)

    def local_ids(block, column):
        ids = jnp.broadcast_to(cand[column : column + 1, :], square)
        ids = jnp.sum(jnp.where(same, ids, 0.0), axis=1, keepdims=True)
        local = ids - (block * class_block).astype(jnp.float32)
        inside = (local >= 0.0) & (local < class_block)
        return jnp.broadcast_to(jnp.where(inside, local, -1.0), (part_dev, cycles))

    def extras(block):
        return jnp.concatenate([quad, quad, local_ids(block, 0), local_ids(block, 1)], axis=1)

    for turn in range(ROTATIONS):
        piece = images_vmem[:, turn * shift : (turn + 1) * shift].astype(jnp.float32) * factor
        piece = piece.astype(jnp.bfloat16).astype(jnp.float32)
        own_wide[turn * part_dev : (turn + 1) * part_dev, :] = piece
    own_wide[rows : rows + 16, :] = jnp.zeros((16, shift), jnp.float32)
    own_wide[rows : rows + part_dev, :] = extras(1 - side)
    own_send[...] = own_wide[...].astype(jnp.bfloat16)

    pl.semaphore_wait(barrier, doms)
    swap = pltpu.make_async_remote_copy(
        src_ref=own_send,
        dst_ref=other_recv,
        send_sem=pair_send_sem.at[0],
        recv_sem=pair_recv_sem.at[0],
        device_id={"cls": 1 - side},
        device_id_type=MESH,
    )
    swap.start()

    loads[4].wait()
    energy = jnp.zeros((class_block, LANES), jnp.float32)
    for start in range(0, features, LANES):
        part = held[:, start : start + LANES].astype(jnp.float32)
        energy = energy + part * part

    def frame(values, framed):
        doubled = jnp.concatenate([values, values], axis=0)
        for late in range(4):
            cut = late * part_dev
            moved = jnp.concatenate([doubled[cut:], doubled[:cut]], axis=0) if cut else doubled
            twins[late] = moved.astype(jnp.bfloat16)
        for turn in range(ROTATIONS):
            begin = turn // 4 * 4 * part_dev
            framed[:, turn * shift : (turn + 1) * shift] = twins[turn % 4, begin : begin + rows, :]

    contract_last = (((1,), (1,)), ((), ()))
    lane = lax.broadcasted_iota(jnp.int32, (part_dev, rows), 1)
    own_lane = (lane & (part_dev - 1)) == lax.broadcasted_iota(jnp.int32, (part_dev, rows), 0)
    class_row = lax.broadcasted_iota(jnp.int32, (class_block, rows), 0).astype(jnp.float32)

    def score(framed, info):
        cross = lax.dot_general(
            held[...], framed[...], contract_last, preferred_element_type=jnp.float32
        )
        norm = lax.dot_general(
            energy,
            jnp.concatenate([info[:, :LANES]] * ROTATIONS, axis=0),
            contract_last,
            precision=lax.Precision.HIGHEST,
            preferred_element_type=jnp.float32,
        )
        logits = cross - 0.5 * norm
        found = []
        for place in range(TOP_CAND):
            ids = info[:, (2 + place) * cycles : (2 + place) * cycles + 1]
            wanted = jnp.sum(jnp.where(own_lane, ids, 0.0), axis=0, keepdims=True)
            value = jnp.sum(jnp.where(class_row == wanted, logits, 0.0), axis=0, keepdims=True)
            live = own_lane & (ids >= 0.0)
            found.append((live, jnp.where(live, value, NEGATIVE)))
        peak = functools.reduce(jnp.maximum, [value for live, value in found])
        peak = jnp.max(peak, axis=1, keepdims=True)
        total = sum(jnp.where(live, jnp.exp(value - peak), 0.0) for live, value in found)
        return found, peak, jnp.sum(total, axis=1, keepdims=True)

    own_info = extras(side)
    frame(own_wide[:rows, :], own_framed)
    own_found, own_peak, own_total = score(own_framed, own_info)

    swap.wait()
    other_all = other_recv[...].astype(jnp.float32)
    other_info = other_all[rows : rows + part_dev, :]
    by_pair = [own_info, own_info, other_info, other_info]
    ids_send[...] = jnp.concatenate(
        [
            jnp.broadcast_to(
                info[:, (2 + place % 2) * cycles : (2 + place % 2) * cycles + 1], (part_dev, LANES)
            )
            for place, info in enumerate(by_pair)
        ],
        axis=0,
    ).astype(jnp.bfloat16)
    mine = pl.ds(pl.multiple_of(me * pairs, pairs), pairs)
    ids_recv[mine, :] = ids_send[...]
    id_copies = []
    for step, peer in enumerate(peers):
        copy = pltpu.make_async_remote_copy(
            src_ref=ids_send,
            dst_ref=ids_recv.at[mine, :],
            send_sem=ids_send_sem.at[step],
            recv_sem=ids_recv_sem.at[step],
            device_id={"dom": peer},
            device_id_type=MESH,
        )
        copy.start()
        id_copies.append(copy)

    frame(other_all[:rows, :], other_framed)
    other_found, other_peak, other_total = score(other_framed, other_info)
    peak = jnp.concatenate([own_peak, other_peak], axis=0)
    total = jnp.concatenate([own_total, other_total], axis=0)
    half = lax.broadcasted_iota(jnp.int32, (group, LANES), 1) < LANES // 2
    part_send[...] = jnp.where(half, peak, total)
    share_part = pltpu.make_async_remote_copy(
        src_ref=part_send,
        dst_ref=part_recv,
        send_sem=pair_send_sem.at[1],
        recv_sem=pair_recv_sem.at[1],
        device_id={"cls": 1 - side},
        device_id_type=MESH,
    )
    share_part.start()
    share_part.wait()
    theirs = part_recv[...]
    theirs = jnp.concatenate([theirs[part_dev:, :], theirs[:part_dev, :]], axis=0)
    their_peak = theirs[:, :1]
    their_total = theirs[:, LANES // 2 : LANES // 2 + 1]
    top = jnp.maximum(peak, their_peak)
    both = total * jnp.exp(peak - top) + their_total * jnp.exp(their_peak - top)
    evidence = top + jnp.log(both)
    corner = lax.broadcasted_iota(jnp.int32, (group, LANES), 1) == lax.broadcasted_iota(
        jnp.int32, (group, LANES), 0
    )
    evidence_row = jnp.sum(jnp.where(corner, evidence, 0.0), axis=0, keepdims=True)
    evidence_ref[...] = evidence_row[:, :part_dev]

    def posteriors(found, evidence):
        parts = [jnp.where(live, jnp.exp(value - evidence), 0.0) for live, value in found]
        return jnp.concatenate(parts, axis=0).astype(jnp.bfloat16)

    own_post = posteriors(own_found, evidence[:part_dev])
    other_post = posteriors(other_found, evidence[part_dev:])
    weight = jnp.concatenate(
        [
            jnp.sum(post.astype(jnp.float32), axis=1, keepdims=True)
            for post in (own_post, other_post)
        ],
        axis=0,
    )
    filters = weight * jnp.concatenate([info[:, :cycles] for info in by_pair], axis=0)

    chips = doms // 2
    chip, core = me // 2, lax.rem(me, 2)
    copies = []
    for step in sorted(range(chips), key=lambda step: -min(step, chips - step)):
        target = lax.rem(chip + step, chips)
        lanes = pl.ds(pl.multiple_of(target * 2 * share, LANES), 2 * share)
        terms = jnp.concatenate(
            [
                jnp.dot(own_post, own_framed[:, lanes], preferred_element_type=jnp.float32),
                jnp.dot(other_post, other_framed[:, lanes], preferred_element_type=jnp.float32),
            ],
            axis=0,
        )
        for to in range(2):
            here = pl.ds(pl.multiple_of((2 * target + to) * pairs, pairs), pairs)
            stage[here, :] = jnp.concatenate(
                [terms[:, to * share : (to + 1) * share], filters], axis=1
            ).astype(jnp.bfloat16)
        for to in range(2 if step else 1):
            peer = 2 * target + to if step else me + 1 - 2 * core
            copy = pltpu.make_async_remote_copy(
                src_ref=stage.at[pl.ds(pl.multiple_of(peer * pairs, pairs), pairs), :],
                dst_ref=arrived.at[mine, :],
                send_sem=data_send_sem.at[2 * step + to],
                recv_sem=data_recv_sem.at[2 * step + core if step else 0],
                device_id={"dom": peer},
                device_id_type=MESH,
            )
            copy.start()
            copies.append((copy, 2 * step + to, peer))
    arrived[mine, :] = stage[mine, :]

    for copy in id_copies:
        copy.wait()
    ids = jnp.broadcast_to(
        ids_recv[...].astype(jnp.float32)[:, :1], (doms * pairs, class_block)
    )
    column = lax.broadcasted_iota(jnp.int32, (doms * pairs, class_block), 1).astype(jnp.float32)
    chosen_ref[...] = jnp.where(ids == column, 1.0, 0.0).astype(jnp.bfloat16)
    for copy, place, peer in copies:
        copy.wait_send()
        pltpu.make_async_remote_copy(
            src_ref=stage.at[mine, :],
            dst_ref=arrived.at[mine, :],
            send_sem=data_send_sem.at[place],
            recv_sem=data_recv_sem.at[place],
            device_id={"dom": peer},
            device_id_type=MESH,
        ).wait_recv()


def sums_kernel(arrived, chosen, evidence_in, sums_ref, weight_ref, evidence_ref):
    share = sums_ref.shape[1]
    cycles = weight_ref.shape[0]
    contract_first = (((0,), (0,)), ((), ()))
    evidence_ref[...] = evidence_in[...]
    sums = lax.dot_general(
        chosen[...], arrived[...], contract_first, preferred_element_type=jnp.float32
    )
    sums_ref[...] = sums[:, :share]
    filter_sums = lax.dot_general(
        arrived[:, share - cycles :],
        chosen[...],
        contract_first,
        preferred_element_type=jnp.float32,
    )
    weight_ref[...] = filter_sums[cycles:, :]


def paired_shards(images, ctf, inv_noise, classes, candidates):
    doms = lax.axis_size("dom")
    part_dev, features = images.shape
    cycles = ctf.shape[1]
    class_block = classes.shape[0]
    shift = features // ROTATIONS
    group = 2 * part_dev
    rows = ROTATIONS * part_dev
    pairs = TOP_CAND * group
    share = features // doms
    wide = share + cycles
    own_rows = rows + 16
    f32, bf16 = jnp.float32, jnp.bfloat16
    vmem = pl.BlockSpec(memory_space=pltpu.VMEM)
    arrived, chosen, evidence = pl.pallas_call(
        functools.partial(estep_kernel, doms),
        out_shape=(
            jax.ShapeDtypeStruct((doms * pairs, wide), bf16),
            jax.ShapeDtypeStruct((doms * pairs, class_block), bf16),
            jax.ShapeDtypeStruct((1, part_dev), f32),
        ),
        in_specs=[pl.BlockSpec(memory_space=pltpu.HBM)] * 5,
        out_specs=(vmem, vmem, vmem),
        scratch_shapes=[
            pltpu.VMEM((class_block, features), bf16),
            pltpu.VMEM((part_dev, features), bf16),
            pltpu.VMEM((part_dev, cycles), f32),
            pltpu.VMEM((1, cycles), f32),
            pltpu.VMEM((TOP_CAND, part_dev), jnp.int32),
            pltpu.VMEM((own_rows, shift), f32),
            pltpu.VMEM((own_rows, shift), bf16),
            pltpu.VMEM((own_rows, shift), bf16),
            pltpu.VMEM((4, 2 * rows, shift), bf16),
            pltpu.VMEM((rows, features), bf16),
            pltpu.VMEM((rows, features), bf16),
            pltpu.VMEM((group, LANES), f32),
            pltpu.VMEM((group, LANES), f32),
            pltpu.VMEM((pairs, LANES), bf16),
            pltpu.VMEM((doms * pairs, LANES), bf16),
            pltpu.VMEM((doms * pairs, wide), bf16),
            pltpu.SemaphoreType.DMA((5,)),
            pltpu.SemaphoreType.DMA((2,)),
            pltpu.SemaphoreType.DMA((2,)),
            pltpu.SemaphoreType.DMA((doms - 1,)),
            pltpu.SemaphoreType.DMA((doms - 1,)),
            pltpu.SemaphoreType.DMA((doms,)),
            pltpu.SemaphoreType.DMA((doms,)),
        ],
        compiler_params=pltpu.CompilerParams(
            collective_id=0, has_side_effects=True, vmem_limit_bytes=63 * 1024 * 1024
        ),
    )(images, ctf, inv_noise[None, :], candidates.T, classes)
    sums, weight, evidence = pl.pallas_call(
        sums_kernel,
        out_shape=(
            jax.ShapeDtypeStruct((class_block, share), f32),
            jax.ShapeDtypeStruct((cycles, class_block), f32),
            jax.ShapeDtypeStruct((1, part_dev), f32),
        ),
        in_specs=[vmem] * 3,
        out_specs=(vmem, vmem, vmem),
        compiler_params=pltpu.CompilerParams(vmem_limit_bytes=63 * 1024 * 1024),
    )(arrived, chosen, evidence)
    return sums.T, weight.T, evidence.reshape(part_dev)


def pick_plan(images, ctf, inv_noise, classes, candidates):
    doms = lax.axis_size("dom")
    part_dev, features = images.shape
    cycles = ctf.shape[1]
    fits = (
        lax.axis_size("cls") == 2
        and part_dev == 4
        and 2 * cycles == LANES
        and features == ROTATIONS * 2 * LANES
        and doms % 2 == 0
        and (features // doms) % LANES == cycles
        and classes.shape[0] <= 256
    )
    plan = paired_shards if fits else shards
    return plan(images, ctf, inv_noise, classes, candidates)


def solution(mesh):
    in_specs = (
        P(("dom", "cls"), None),
        P(("dom", "cls"), None),
        P(),
        P("cls", None),
        P(("dom", "cls"), None),
    )
    out_specs = (P("dom", "cls"), P("cls", None), P(("dom", "cls")))
    return jax.shard_map(
        pick_plan, mesh=mesh, in_specs=in_specs, out_specs=out_specs, check_vma=False
    )
```

```python
import functools
import math

import jax
import jax.numpy as jnp
from jax import lax
from jax.experimental import pallas as pl
from jax.experimental.pallas import tpu as pltpu
from jax.sharding import PartitionSpec as P

ANGLES = 72
ROTATIONS = 36
TOP_CAND = 2


NEGATIVE = -1e30


def combined_all(value, axis, join):
    pieces = jax.tree.map(lambda part: lax.all_gather(part, axis), value)
    head = jax.tree.map(lambda part: part[0], pieces)
    tail = jax.tree.map(lambda part: part[1:], pieces)
    subtotal, _ = lax.scan(lambda subtotal, section: (join(subtotal, section), None), head, tail)
    return subtotal


def combine_totals(earlier, later):
    highest = jnp.maximum(earlier[0], later[0])
    return (
        highest,
        earlier[1] * jnp.exp(earlier[0] - highest) + later[1] * jnp.exp(later[0] - highest),
    )


def shards(images, ctf, inv_noise, classes, candidates):
    cls_count = lax.axis_size("cls")
    my_index = lax.axis_index("cls")
    part_dev = images.shape[0]
    class_block = classes.shape[0]
    features = images.shape[1]
    cycles = ctf.shape[1]
    capacity = min(5 * part_dev * TOP_CAND // (2 * cls_count), part_dev)
    group_size = cls_count * part_dev
    shift = features // ANGLES * (ANGLES // ROTATIONS)
    turn_ids = jnp.arange(ROTATIONS, dtype=jnp.int32)
    ctf_noise = ctf * inv_noise[None, :]
    weighted = (images.astype(jnp.float32) * jnp.tile(ctf_noise, (1, features // cycles))).astype(
        jnp.bfloat16
    )
    quadratic = (ctf * ctf * inv_noise[None, :]).astype(jnp.bfloat16)
    everyone = lax.all_gather(candidates, "cls", axis=0, tiled=True)
    block_ids = jnp.arange(class_block, dtype=jnp.int32) + my_index * class_block
    cand_mask = jnp.any(everyone[:, :, None] == block_ids[None, None, :], axis=1).astype(
        jnp.float32
    )
    owner_ids = jnp.arange(cls_count, dtype=jnp.int32)
    routed = jnp.any(
        (everyone // class_block)[:, :, None] == owner_ids[None, None, :], axis=1
    ).astype(jnp.int32)
    by_source = routed.reshape(cls_count, part_dev, cls_count)
    slot_of = jnp.cumsum(by_source, axis=1) - by_source
    slot_ids = jnp.arange(capacity, dtype=jnp.int32)
    mine_routed = lax.dynamic_index_in_dim(by_source, my_index, 0, keepdims=False)
    mine_slot = lax.dynamic_index_in_dim(slot_of, my_index, 0, keepdims=False)
    packing = (mine_routed.T[:, None, :] == 1) & (
        mine_slot.T[:, None, :] == slot_ids[None, :, None]
    )
    packing = packing.reshape(cls_count * capacity, part_dev).astype(jnp.bfloat16)
    send_data = jnp.dot(packing, weighted, preferred_element_type=jnp.float32).astype(jnp.bfloat16)
    send_quad = jnp.dot(packing, quadratic, preferred_element_type=jnp.float32).astype(jnp.bfloat16)
    row_data, row_quad = (
        lax.all_to_all(send_data, "cls", split_axis=0, concat_axis=0, tiled=True),
        lax.all_to_all(send_quad, "cls", split_axis=0, concat_axis=0, tiled=True),
    )
    into_mine = lax.dynamic_index_in_dim(by_source, my_index, 2, keepdims=False)
    slot_mine = lax.dynamic_index_in_dim(slot_of, my_index, 2, keepdims=False)
    selected = (into_mine[:, None, :] == 1) & (slot_mine[:, None, :] == slot_ids[None, :, None])
    diagonal = jnp.eye(cls_count, dtype=jnp.float32)
    unpack = (selected.astype(jnp.float32)[:, :, None, :] * diagonal[:, None, :, None]).reshape(
        cls_count * capacity, group_size
    )
    row_mask = jnp.dot(unpack, cand_mask, precision=lax.Precision.HIGHEST)
    row_count = row_data.shape[0]
    energy = jnp.sum(
        jnp.square(classes.astype(jnp.float32)).reshape(class_block, features // cycles, cycles),
        axis=1,
    )
    quad_wide = row_quad.astype(jnp.float32)
    norm_term = jnp.dot(quad_wide, energy.T, precision=lax.Precision.HIGHEST)
    twin_classes = jnp.concatenate([classes, classes], axis=1)
    feat_block = math.gcd(features, 1152)

    def add_block(block_index, running):
        offset = block_index * feat_block
        rotated = jax.vmap(
            lambda rotation: lax.dynamic_slice_in_dim(
                twin_classes, offset - rotation * shift + features, feat_block, 1
            )
        )(turn_ids)
        section = lax.dynamic_slice_in_dim(row_data, offset, feat_block, 1)
        return running + lax.dot_general(
            section, rotated, (((1,), (2,)), ((), ())), preferred_element_type=jnp.float32
        )

    cross = lax.fori_loop(
        0,
        features // feat_block,
        add_block,
        jnp.zeros((row_count, ROTATIONS, class_block), jnp.float32),
    )
    logits = cross - 0.5 * norm_term[:, None, :]
    live = jnp.broadcast_to(row_mask[:, None, :] > 0.5, logits.shape)
    masked = jnp.where(live, logits, NEGATIVE)
    peak = jnp.max(masked, axis=(1, 2))
    part_total = jnp.sum(jnp.where(live, jnp.exp(masked - peak[:, None, None]), 0.0), axis=(1, 2))
    group_peak = jnp.max(jnp.where(unpack > 0.5, peak[:, None], NEGATIVE), axis=0)
    group_total = jnp.sum(unpack * part_total[:, None], axis=0)
    top_all, total_all = combined_all((group_peak, group_total), "cls", combine_totals)
    group_evidence = top_all + jnp.log(total_all)
    own_evidence = lax.dynamic_slice_in_dim(group_evidence, my_index * part_dev, part_dev, 0)
    row_evidence = jnp.dot(unpack, group_evidence, precision=lax.Precision.HIGHEST)
    posterior = jnp.where(live, jnp.exp(logits - row_evidence[:, None, None]), 0.0).astype(
        jnp.bfloat16
    )
    weight_total = jnp.sum(posterior.astype(jnp.float32), axis=1)
    ctf_part = jnp.dot(weight_total.T, quad_wide, precision=lax.Precision.HIGHEST)
    weight_sums = lax.psum(ctf_part, "dom")
    twin_rows = jnp.concatenate([row_data, row_data], axis=1)

    def add_sums(block_index, running):
        offset = block_index * feat_block
        stacked = jax.vmap(
            lambda rotation: lax.dynamic_slice_in_dim(
                twin_rows, offset + rotation * shift, feat_block, 1
            )
        )(turn_ids)
        block_sum = lax.dot_general(
            posterior, stacked, (((0, 1), (1, 0)), ((), ())), preferred_element_type=jnp.float32
        )
        return lax.dynamic_update_slice_in_dim(running, block_sum, offset, 1)

    summed = lax.fori_loop(
        0, features // feat_block, add_sums, jnp.zeros((class_block, features), jnp.float32)
    )
    full_term = summed.T
    class_sums = lax.psum_scatter(full_term, "dom", scatter_dimension=0, tiled=True)
    return (class_sums, weight_sums, own_evidence)


MESH = pl.DeviceIdType.MESH
LANES = 128


def estep_kernel(
    doms,
    images_ref,
    ctf_ref,
    noise_ref,
    cand_ref,
    classes_ref,
    arrived,
    chosen_ref,
    evidence_ref,
    held,
    images_vmem,
    ctf_vmem,
    noise_vmem,
    cand_vmem,
    own_wide,
    own_send,
    other_recv,
    twins,
    own_framed,
    other_framed,
    part_send,
    part_recv,
    ids_send,
    ids_recv,
    stage,
    load_sem,
    pair_send_sem,
    pair_recv_sem,
    ids_send_sem,
    ids_recv_sem,
    data_send_sem,
    data_recv_sem,
    next_send_sem,
    next_recv_sem,
):
    me = lax.axis_index("dom")
    side = lax.axis_index("cls")
    part_dev, features = images_ref.shape
    cycles = ctf_ref.shape[1]
    class_block = held.shape[0]
    shift = features // ROTATIONS
    group = 2 * part_dev
    pairs = TOP_CAND * group
    rows = ROTATIONS * part_dev
    share = features // doms
    peers = [lax.rem(me + step, doms) for step in range(1, doms)]

    loads = [
        pltpu.make_async_copy(source, target, load_sem.at[place])
        for place, (source, target) in enumerate(
            [
                (cand_ref, cand_vmem),
                (noise_ref, noise_vmem),
                (ctf_ref, ctf_vmem),
                (images_ref, images_vmem),
                (classes_ref, held),
            ]
        )
    ]
    for load in loads:
        load.start()
    barrier = pltpu.get_barrier_semaphore()
    pl.semaphore_signal(barrier, inc=1, device_id={"cls": 1 - side}, device_id_type=MESH)
    for peer in peers:
        pl.semaphore_signal(barrier, inc=1, device_id={"dom": peer}, device_id_type=MESH)

    for load in loads[:4]:
        load.wait()
    ctf = ctf_vmem[...]
    noise = noise_vmem[...]
    factor = jnp.concatenate([ctf * noise] * (shift // cycles), axis=1)
    quad = (ctf * ctf * noise).astype(jnp.bfloat16).astype(jnp.float32)
    cand = cand_vmem[...].astype(jnp.float32)
    square = (part_dev, part_dev)
    same = lax.broadcasted_iota(jnp.int32, square, 0) == lax.broadcasted_iota(jnp.int32, square, 1)

    def local_ids(block, column):
        ids = jnp.broadcast_to(cand[column : column + 1, :], square)
        ids = jnp.sum(jnp.where(same, ids, 0.0), axis=1, keepdims=True)
        local = ids - (block * class_block).astype(jnp.float32)
        inside = (local >= 0.0) & (local < class_block)
        return jnp.broadcast_to(jnp.where(inside, local, -1.0), (part_dev, cycles))

    def extras(block):
        return jnp.concatenate([quad, quad, local_ids(block, 0), local_ids(block, 1)], axis=1)

    for turn in range(ROTATIONS):
        piece = images_vmem[:, turn * shift : (turn + 1) * shift].astype(jnp.float32) * factor
        piece = piece.astype(jnp.bfloat16).astype(jnp.float32)
        own_wide[turn * part_dev : (turn + 1) * part_dev, :] = piece
    own_wide[rows : rows + 16, :] = jnp.zeros((16, shift), jnp.float32)
    own_wide[rows : rows + part_dev, :] = extras(1 - side)
    own_send[...] = own_wide[...].astype(jnp.bfloat16)

    pl.semaphore_wait(barrier, doms)
    swap = pltpu.make_async_remote_copy(
        src_ref=own_send,
        dst_ref=other_recv,
        send_sem=pair_send_sem.at[0],
        recv_sem=pair_recv_sem.at[0],
        device_id={"cls": 1 - side},
        device_id_type=MESH,
    )
    swap.start()

    loads[4].wait()
    energy = jnp.zeros((class_block, LANES), jnp.float32)
    for start in range(0, features, LANES):
        part = held[:, start : start + LANES].astype(jnp.float32)
        energy = energy + part * part

    def frame(values, framed):
        doubled = jnp.concatenate([values, values], axis=0)
        for late in range(4):
            cut = late * part_dev
            moved = jnp.concatenate([doubled[cut:], doubled[:cut]], axis=0) if cut else doubled
            twins[late] = moved.astype(jnp.bfloat16)
        for turn in range(ROTATIONS):
            begin = turn // 4 * 4 * part_dev
            framed[:, turn * shift : (turn + 1) * shift] = twins[turn % 4, begin : begin + rows, :]

    contract_last = (((1,), (1,)), ((), ()))
    lane = lax.broadcasted_iota(jnp.int32, (part_dev, rows), 1)
    own_lane = (lane & (part_dev - 1)) == lax.broadcasted_iota(jnp.int32, (part_dev, rows), 0)
    class_row = lax.broadcasted_iota(jnp.int32, (class_block, rows), 0).astype(jnp.float32)

    def score(framed, info):
        cross = lax.dot_general(
            held[...], framed[...], contract_last, preferred_element_type=jnp.float32
        )
        norm = lax.dot_general(
            energy,
            jnp.concatenate([info[:, :LANES]] * ROTATIONS, axis=0),
            contract_last,
            precision=lax.Precision.HIGHEST,
            preferred_element_type=jnp.float32,
        )
        logits = cross - 0.5 * norm
        values = []
        for place in range(TOP_CAND):
            ids = info[:, (2 + place) * cycles : (2 + place) * cycles + 1]
            wanted = jnp.sum(jnp.where(own_lane, ids, 0.0), axis=0, keepdims=True)
            values.append(
                jnp.sum(jnp.where(class_row == wanted, logits, 0.0), axis=0, keepdims=True)
            )
        return values

    own_info = extras(side)
    frame(own_wide[:rows, :], own_framed)
    own_values = score(own_framed, own_info)

    swap.wait()
    other_all = other_recv[...].astype(jnp.float32)
    other_info = other_all[rows : rows + part_dev, :]
    by_pair = [own_info, own_info, other_info, other_info]
    ids_send[...] = jnp.concatenate(
        [
            jnp.broadcast_to(
                info[:, (2 + place % 2) * cycles : (2 + place % 2) * cycles + 1], (part_dev, LANES)
            )
            for place, info in enumerate(by_pair)
        ],
        axis=0,
    ).astype(jnp.bfloat16)
    mine = pl.ds(pl.multiple_of(me * pairs, pairs), pairs)
    ids_recv[mine, :] = ids_send[...]
    id_copies = []
    for step, peer in enumerate(peers):
        copy = pltpu.make_async_remote_copy(
            src_ref=ids_send,
            dst_ref=ids_recv.at[mine, :],
            send_sem=ids_send_sem.at[step],
            recv_sem=ids_recv_sem.at[step],
            device_id={"dom": peer},
            device_id_type=MESH,
        )
        copy.start()
        id_copies.append(copy)

    frame(other_all[:rows, :], other_framed)
    other_values = score(other_framed, other_info)
    upper = lax.broadcasted_iota(jnp.int32, part_send.shape, 0) == 0
    part_send[...] = jnp.where(upper, other_values[0], other_values[1])
    share_part = pltpu.make_async_remote_copy(
        src_ref=part_send,
        dst_ref=part_recv,
        send_sem=pair_send_sem.at[1],
        recv_sem=pair_recv_sem.at[1],
        device_id={"cls": 1 - side},
        device_id_type=MESH,
    )
    share_part.start()
    share_part.wait()
    theirs = part_recv[...]
    first = jnp.where(own_lane, own_values[0] + theirs[0:1, :], NEGATIVE)
    second = jnp.where(own_lane, own_values[1] + theirs[1:2, :], NEGATIVE)
    peak = jnp.max(jnp.maximum(first, second), axis=1, keepdims=True)
    total = jnp.where(own_lane, jnp.exp(first - peak) + jnp.exp(second - peak), 0.0)
    evidence = peak + jnp.log(jnp.sum(total, axis=1, keepdims=True))
    corner = lax.broadcasted_iota(jnp.int32, (part_dev, LANES), 1) == lax.broadcasted_iota(
        jnp.int32, (part_dev, LANES), 0
    )
    evidence_row = jnp.sum(jnp.where(corner, evidence, 0.0), axis=0, keepdims=True)
    evidence_ref[...] = evidence_row[:, :part_dev]

    posterior = jnp.concatenate(
        [jnp.where(own_lane, jnp.exp(value - evidence), 0.0) for value in (first, second)], axis=0
    ).astype(jnp.bfloat16)
    weight = jnp.sum(posterior.astype(jnp.float32), axis=1, keepdims=True)
    filters = weight * jnp.concatenate([quad, quad], axis=0)

    chips = doms // 2
    chip, core = me // 2, lax.rem(me, 2)

    def across(step):
        place, bit = 0, 1
        while bit < chips:
            digit = lax.rem(chip // bit, 2)
            place = place + bit * (1 - digit if step & bit else digit)
            bit *= 2
        return place

    def to_dom(peer, place, landing):
        return pltpu.make_async_remote_copy(
            src_ref=stage.at[peer],
            dst_ref=arrived.at[me],
            send_sem=data_send_sem.at[place],
            recv_sem=data_recv_sem.at[landing],
            device_id={"dom": peer},
            device_id_type=MESH,
        )

    def to_side(source, place, target):
        return pltpu.make_async_remote_copy(
            src_ref=source,
            dst_ref=arrived.at[doms + target],
            send_sem=next_send_sem.at[place],
            recv_sem=next_recv_sem.at[place],
            device_id={"cls": 1 - side},
            device_id_type=MESH,
        )

    half = chips // 2
    order = [step for near in range(1, half) for step in (half + near - 1, near)]
    order += [chips - 1, 0]
    copies = []
    for step in order:
        target = across(step)
        lanes = pl.ds(pl.multiple_of(target * 2 * share, LANES), 2 * share)
        terms = jnp.dot(posterior, own_framed[:, lanes], preferred_element_type=jnp.float32)
        for to in range(2):
            stage[2 * target + to] = jnp.concatenate(
                [terms[:, to * share : (to + 1) * share], filters], axis=1
            ).astype(jnp.bfloat16)
        for to in range(2 if step else 1):
            peer = 2 * target + to if step else me + 1 - 2 * core
            landing = 2 * step + core if step else 0
            copy = to_dom(peer, 2 * step + to, landing)
            copy.start()
            copies.append((copy, peer, 2 * step + to))
    mine_next = to_side(stage.at[me], doms - 1, me)
    mine_next.start()
    arrived[me] = stage[me]

    nexts = [mine_next]
    for place, (copy, peer, landing) in enumerate(copies):
        to_dom(peer, landing, landing).wait_recv()
        onward = to_side(arrived.at[peer], place, peer)
        onward.start()
        nexts.append(onward)

    for copy in id_copies:
        copy.wait()
    ids = ids_recv[...].astype(jnp.float32)
    count = doms * pairs // 2
    for place in range(2):
        part = [
            ids[dom * pairs + place * group : dom * pairs + (place + 1) * group, :1]
            for dom in range(doms)
        ]
        part = jnp.broadcast_to(jnp.concatenate(part, axis=0), (count, class_block))
        column = lax.broadcasted_iota(jnp.int32, (count, class_block), 1).astype(jnp.float32)
        chosen_ref[place * count : (place + 1) * count, :] = jnp.where(
            part == column, 1.0, 0.0
        ).astype(jnp.bfloat16)
    for copy, peer, landing in copies:
        copy.wait_send()
    for onward in nexts:
        onward.wait()


def sums_kernel(arrived, chosen, evidence_in, sums_ref, weight_ref, evidence_ref):
    share = sums_ref.shape[1]
    cycles = weight_ref.shape[0]
    contract_first = (((0,), (0,)), ((), ()))
    evidence_ref[...] = evidence_in[...]
    sums = lax.dot_general(
        chosen[...], arrived[...], contract_first, preferred_element_type=jnp.float32
    )
    sums_ref[...] = sums[:, :share]
    filter_sums = lax.dot_general(
        arrived[:, share - cycles :],
        chosen[...],
        contract_first,
        preferred_element_type=jnp.float32,
    )
    weight_ref[...] = filter_sums[cycles:, :]


def paired_shards(images, ctf, inv_noise, classes, candidates):
    doms = lax.axis_size("dom")
    part_dev, features = images.shape
    cycles = ctf.shape[1]
    class_block = classes.shape[0]
    shift = features // ROTATIONS
    group = 2 * part_dev
    rows = ROTATIONS * part_dev
    pairs = TOP_CAND * group
    share = features // doms
    wide = share + cycles
    own_rows = rows + 16
    f32, bf16 = jnp.float32, jnp.bfloat16
    vmem = pl.BlockSpec(memory_space=pltpu.VMEM)
    arrived, chosen, evidence = pl.pallas_call(
        functools.partial(estep_kernel, doms),
        out_shape=(
            jax.ShapeDtypeStruct((2 * doms, group, wide), bf16),
            jax.ShapeDtypeStruct((doms * pairs, class_block), bf16),
            jax.ShapeDtypeStruct((1, part_dev), f32),
        ),
        in_specs=[pl.BlockSpec(memory_space=pltpu.HBM)] * 5,
        out_specs=(vmem, vmem, vmem),
        scratch_shapes=[
            pltpu.VMEM((class_block, features), bf16),
            pltpu.VMEM((part_dev, features), bf16),
            pltpu.VMEM((part_dev, cycles), f32),
            pltpu.VMEM((1, cycles), f32),
            pltpu.VMEM((TOP_CAND, part_dev), jnp.int32),
            pltpu.VMEM((own_rows, shift), f32),
            pltpu.VMEM((own_rows, shift), bf16),
            pltpu.VMEM((own_rows, shift), bf16),
            pltpu.VMEM((4, 2 * rows, shift), bf16),
            pltpu.VMEM((rows, features), bf16),
            pltpu.VMEM((rows, features), bf16),
            pltpu.VMEM((group, rows), f32),
            pltpu.VMEM((group, rows), f32),
            pltpu.VMEM((pairs, LANES), bf16),
            pltpu.VMEM((doms * pairs, LANES), bf16),
            pltpu.VMEM((doms, group, wide), bf16),
            pltpu.SemaphoreType.DMA((5,)),
            pltpu.SemaphoreType.DMA((2,)),
            pltpu.SemaphoreType.DMA((2,)),
            pltpu.SemaphoreType.DMA((doms - 1,)),
            pltpu.SemaphoreType.DMA((doms - 1,)),
            pltpu.SemaphoreType.DMA((doms,)),
            pltpu.SemaphoreType.DMA((doms,)),
            pltpu.SemaphoreType.DMA((doms,)),
            pltpu.SemaphoreType.DMA((doms,)),
        ],
        compiler_params=pltpu.CompilerParams(
            collective_id=0, has_side_effects=True, vmem_limit_bytes=63 * 1024 * 1024
        ),
    )(images, ctf, inv_noise[None, :], candidates.T, classes)
    sums, weight, evidence = pl.pallas_call(
        sums_kernel,
        out_shape=(
            jax.ShapeDtypeStruct((class_block, share), f32),
            jax.ShapeDtypeStruct((cycles, class_block), f32),
            jax.ShapeDtypeStruct((1, part_dev), f32),
        ),
        in_specs=[vmem] * 3,
        out_specs=(vmem, vmem, vmem),
        compiler_params=pltpu.CompilerParams(vmem_limit_bytes=63 * 1024 * 1024),
    )(arrived.reshape(doms * pairs, wide), chosen, evidence)
    return sums.T, weight.T, evidence.reshape(part_dev)


def pick_plan(images, ctf, inv_noise, classes, candidates):
    doms = lax.axis_size("dom")
    part_dev, features = images.shape
    cycles = ctf.shape[1]
    fits = (
        lax.axis_size("cls") == 2
        and part_dev == 4
        and 2 * cycles == LANES
        and features == ROTATIONS * 2 * LANES
        and doms >= 8
        and doms & (doms - 1) == 0
        and (features // doms) % LANES == cycles
        and classes.shape[0] <= 256
    )
    plan = paired_shards if fits else shards
    return plan(images, ctf, inv_noise, classes, candidates)


def solution(mesh):
    in_specs = (
        P(("dom", "cls"), None),
        P(("dom", "cls"), None),
        P(),
        P("cls", None),
        P(("dom", "cls"), None),
    )
    out_specs = (P("dom", "cls"), P("cls", None), P(("dom", "cls")))
    return jax.shard_map(
        pick_plan, mesh=mesh, in_specs=in_specs, out_specs=out_specs, check_vma=False
    )
```

```python
import functools
import math

import jax
import jax.numpy as jnp
from jax import lax
from jax.experimental import pallas as pl
from jax.experimental.pallas import tpu as pltpu
from jax.sharding import PartitionSpec as P

ANGLES = 72
ROTATIONS = 36
TOP_CAND = 2


NEGATIVE = -1e30


def combined_all(value, axis, join):
    pieces = jax.tree.map(lambda part: lax.all_gather(part, axis), value)
    head = jax.tree.map(lambda part: part[0], pieces)
    tail = jax.tree.map(lambda part: part[1:], pieces)
    subtotal, _ = lax.scan(lambda subtotal, section: (join(subtotal, section), None), head, tail)
    return subtotal


def combine_totals(earlier, later):
    highest = jnp.maximum(earlier[0], later[0])
    return (
        highest,
        earlier[1] * jnp.exp(earlier[0] - highest) + later[1] * jnp.exp(later[0] - highest),
    )


def shards(images, ctf, inv_noise, classes, candidates):
    cls_count = lax.axis_size("cls")
    my_index = lax.axis_index("cls")
    part_dev = images.shape[0]
    class_block = classes.shape[0]
    features = images.shape[1]
    cycles = ctf.shape[1]
    capacity = min(5 * part_dev * TOP_CAND // (2 * cls_count), part_dev)
    group_size = cls_count * part_dev
    shift = features // ANGLES * (ANGLES // ROTATIONS)
    turn_ids = jnp.arange(ROTATIONS, dtype=jnp.int32)
    ctf_noise = ctf * inv_noise[None, :]
    weighted = (images.astype(jnp.float32) * jnp.tile(ctf_noise, (1, features // cycles))).astype(
        jnp.bfloat16
    )
    quadratic = (ctf * ctf * inv_noise[None, :]).astype(jnp.bfloat16)
    everyone = lax.all_gather(candidates, "cls", axis=0, tiled=True)
    block_ids = jnp.arange(class_block, dtype=jnp.int32) + my_index * class_block
    cand_mask = jnp.any(everyone[:, :, None] == block_ids[None, None, :], axis=1).astype(
        jnp.float32
    )
    owner_ids = jnp.arange(cls_count, dtype=jnp.int32)
    routed = jnp.any(
        (everyone // class_block)[:, :, None] == owner_ids[None, None, :], axis=1
    ).astype(jnp.int32)
    by_source = routed.reshape(cls_count, part_dev, cls_count)
    slot_of = jnp.cumsum(by_source, axis=1) - by_source
    slot_ids = jnp.arange(capacity, dtype=jnp.int32)
    mine_routed = lax.dynamic_index_in_dim(by_source, my_index, 0, keepdims=False)
    mine_slot = lax.dynamic_index_in_dim(slot_of, my_index, 0, keepdims=False)
    packing = (mine_routed.T[:, None, :] == 1) & (
        mine_slot.T[:, None, :] == slot_ids[None, :, None]
    )
    packing = packing.reshape(cls_count * capacity, part_dev).astype(jnp.bfloat16)
    send_data = jnp.dot(packing, weighted, preferred_element_type=jnp.float32).astype(jnp.bfloat16)
    send_quad = jnp.dot(packing, quadratic, preferred_element_type=jnp.float32).astype(jnp.bfloat16)
    row_data, row_quad = (
        lax.all_to_all(send_data, "cls", split_axis=0, concat_axis=0, tiled=True),
        lax.all_to_all(send_quad, "cls", split_axis=0, concat_axis=0, tiled=True),
    )
    into_mine = lax.dynamic_index_in_dim(by_source, my_index, 2, keepdims=False)
    slot_mine = lax.dynamic_index_in_dim(slot_of, my_index, 2, keepdims=False)
    selected = (into_mine[:, None, :] == 1) & (slot_mine[:, None, :] == slot_ids[None, :, None])
    diagonal = jnp.eye(cls_count, dtype=jnp.float32)
    unpack = (selected.astype(jnp.float32)[:, :, None, :] * diagonal[:, None, :, None]).reshape(
        cls_count * capacity, group_size
    )
    row_mask = jnp.dot(unpack, cand_mask, precision=lax.Precision.HIGHEST)
    row_count = row_data.shape[0]
    energy = jnp.sum(
        jnp.square(classes.astype(jnp.float32)).reshape(class_block, features // cycles, cycles),
        axis=1,
    )
    quad_wide = row_quad.astype(jnp.float32)
    norm_term = jnp.dot(quad_wide, energy.T, precision=lax.Precision.HIGHEST)
    twin_classes = jnp.concatenate([classes, classes], axis=1)
    feat_block = math.gcd(features, 1152)

    def add_block(block_index, running):
        offset = block_index * feat_block
        rotated = jax.vmap(
            lambda rotation: lax.dynamic_slice_in_dim(
                twin_classes, offset - rotation * shift + features, feat_block, 1
            )
        )(turn_ids)
        section = lax.dynamic_slice_in_dim(row_data, offset, feat_block, 1)
        return running + lax.dot_general(
            section, rotated, (((1,), (2,)), ((), ())), preferred_element_type=jnp.float32
        )

    cross = lax.fori_loop(
        0,
        features // feat_block,
        add_block,
        jnp.zeros((row_count, ROTATIONS, class_block), jnp.float32),
    )
    logits = cross - 0.5 * norm_term[:, None, :]
    live = jnp.broadcast_to(row_mask[:, None, :] > 0.5, logits.shape)
    masked = jnp.where(live, logits, NEGATIVE)
    peak = jnp.max(masked, axis=(1, 2))
    part_total = jnp.sum(jnp.where(live, jnp.exp(masked - peak[:, None, None]), 0.0), axis=(1, 2))
    group_peak = jnp.max(jnp.where(unpack > 0.5, peak[:, None], NEGATIVE), axis=0)
    group_total = jnp.sum(unpack * part_total[:, None], axis=0)
    top_all, total_all = combined_all((group_peak, group_total), "cls", combine_totals)
    group_evidence = top_all + jnp.log(total_all)
    own_evidence = lax.dynamic_slice_in_dim(group_evidence, my_index * part_dev, part_dev, 0)
    row_evidence = jnp.dot(unpack, group_evidence, precision=lax.Precision.HIGHEST)
    posterior = jnp.where(live, jnp.exp(logits - row_evidence[:, None, None]), 0.0).astype(
        jnp.bfloat16
    )
    weight_total = jnp.sum(posterior.astype(jnp.float32), axis=1)
    ctf_part = jnp.dot(weight_total.T, quad_wide, precision=lax.Precision.HIGHEST)
    weight_sums = lax.psum(ctf_part, "dom")
    twin_rows = jnp.concatenate([row_data, row_data], axis=1)

    def add_sums(block_index, running):
        offset = block_index * feat_block
        stacked = jax.vmap(
            lambda rotation: lax.dynamic_slice_in_dim(
                twin_rows, offset + rotation * shift, feat_block, 1
            )
        )(turn_ids)
        block_sum = lax.dot_general(
            posterior, stacked, (((0, 1), (1, 0)), ((), ())), preferred_element_type=jnp.float32
        )
        return lax.dynamic_update_slice_in_dim(running, block_sum, offset, 1)

    summed = lax.fori_loop(
        0, features // feat_block, add_sums, jnp.zeros((class_block, features), jnp.float32)
    )
    full_term = summed.T
    class_sums = lax.psum_scatter(full_term, "dom", scatter_dimension=0, tiled=True)
    return (class_sums, weight_sums, own_evidence)


MESH = pl.DeviceIdType.MESH
LANES = 128


def estep_kernel(
    doms,
    images_ref,
    ctf_ref,
    noise_ref,
    cand_ref,
    classes_ref,
    arrived,
    chosen_ref,
    evidence_ref,
    held,
    images_vmem,
    ctf_vmem,
    noise_vmem,
    cand_vmem,
    own_wide,
    own_send,
    other_recv,
    twins,
    own_framed,
    other_framed,
    part_send,
    part_recv,
    ids_send,
    ids_recv,
    stage,
    pair_sums,
    load_sem,
    pair_send_sem,
    pair_recv_sem,
    ids_send_sem,
    ids_recv_sem,
    data_send_sem,
    data_recv_sem,
):
    me = lax.axis_index("dom")
    side = lax.axis_index("cls")
    part_dev, features = images_ref.shape
    cycles = ctf_ref.shape[1]
    class_block = held.shape[0]
    shift = features // ROTATIONS
    group = 2 * part_dev
    pairs = TOP_CAND * group
    rows = ROTATIONS * part_dev
    share = features // doms
    wide = stage.shape[1]
    peers = [lax.rem(me + step, doms) for step in range(1, doms)]

    loads = [
        pltpu.make_async_copy(source, target, load_sem.at[place])
        for place, (source, target) in enumerate(
            [
                (cand_ref, cand_vmem),
                (noise_ref, noise_vmem),
                (ctf_ref, ctf_vmem),
                (images_ref, images_vmem),
                (classes_ref, held),
            ]
        )
    ]
    for load in loads:
        load.start()
    barrier = pltpu.get_barrier_semaphore()
    pl.semaphore_signal(barrier, inc=1, device_id={"cls": 1 - side}, device_id_type=MESH)
    for peer in peers:
        pl.semaphore_signal(barrier, inc=1, device_id={"dom": peer}, device_id_type=MESH)

    for load in loads[:4]:
        load.wait()
    ctf = ctf_vmem[...]
    noise = noise_vmem[...]
    factor = jnp.concatenate([ctf * noise] * (shift // cycles), axis=1)
    quad = (ctf * ctf * noise).astype(jnp.bfloat16).astype(jnp.float32)
    cand = cand_vmem[...].astype(jnp.float32)
    square = (part_dev, part_dev)
    same = lax.broadcasted_iota(jnp.int32, square, 0) == lax.broadcasted_iota(jnp.int32, square, 1)

    def local_ids(block, column):
        ids = jnp.broadcast_to(cand[column : column + 1, :], square)
        ids = jnp.sum(jnp.where(same, ids, 0.0), axis=1, keepdims=True)
        local = ids - (block * class_block).astype(jnp.float32)
        inside = (local >= 0.0) & (local < class_block)
        return jnp.broadcast_to(jnp.where(inside, local, -1.0), (part_dev, cycles))

    def extras(block):
        return jnp.concatenate([quad, quad, local_ids(block, 0), local_ids(block, 1)], axis=1)

    for turn in range(ROTATIONS):
        piece = images_vmem[:, turn * shift : (turn + 1) * shift].astype(jnp.float32) * factor
        piece = piece.astype(jnp.bfloat16).astype(jnp.float32)
        own_wide[turn * part_dev : (turn + 1) * part_dev, :] = piece
    own_wide[rows : rows + 16, :] = jnp.zeros((16, shift), jnp.float32)
    own_wide[rows : rows + part_dev, :] = extras(1 - side)
    own_send[...] = own_wide[...].astype(jnp.bfloat16)

    pl.semaphore_wait(barrier, doms)
    swap = pltpu.make_async_remote_copy(
        src_ref=own_send,
        dst_ref=other_recv,
        send_sem=pair_send_sem.at[0],
        recv_sem=pair_recv_sem.at[0],
        device_id={"cls": 1 - side},
        device_id_type=MESH,
    )
    swap.start()

    loads[4].wait()
    energy = jnp.zeros((class_block, LANES), jnp.float32)
    for start in range(0, features, LANES):
        part = held[:, start : start + LANES].astype(jnp.float32)
        energy = energy + part * part

    def frame(values, framed):
        doubled = jnp.concatenate([values, values], axis=0)
        for late in range(4):
            cut = late * part_dev
            moved = jnp.concatenate([doubled[cut:], doubled[:cut]], axis=0) if cut else doubled
            twins[late] = moved.astype(jnp.bfloat16)
        for turn in range(ROTATIONS):
            begin = turn // 4 * 4 * part_dev
            framed[:, turn * shift : (turn + 1) * shift] = twins[turn % 4, begin : begin + rows, :]

    contract_last = (((1,), (1,)), ((), ()))
    lane = lax.broadcasted_iota(jnp.int32, (part_dev, rows), 1)
    own_lane = (lane & (part_dev - 1)) == lax.broadcasted_iota(jnp.int32, (part_dev, rows), 0)
    class_row = lax.broadcasted_iota(jnp.int32, (class_block, rows), 0).astype(jnp.float32)

    def score(framed, info):
        cross = lax.dot_general(
            held[...], framed[...], contract_last, preferred_element_type=jnp.float32
        )
        norm = lax.dot_general(
            energy,
            jnp.concatenate([info[:, :LANES]] * ROTATIONS, axis=0),
            contract_last,
            precision=lax.Precision.HIGHEST,
            preferred_element_type=jnp.float32,
        )
        logits = cross - 0.5 * norm
        found = []
        for place in range(TOP_CAND):
            ids = info[:, (2 + place) * cycles : (2 + place) * cycles + 1]
            wanted = jnp.sum(jnp.where(own_lane, ids, 0.0), axis=0, keepdims=True)
            value = jnp.sum(jnp.where(class_row == wanted, logits, 0.0), axis=0, keepdims=True)
            live = own_lane & (ids >= 0.0)
            found.append((live, jnp.where(live, value, NEGATIVE)))
        peak = functools.reduce(jnp.maximum, [value for live, value in found])
        peak = jnp.max(peak, axis=1, keepdims=True)
        total = sum(jnp.where(live, jnp.exp(value - peak), 0.0) for live, value in found)
        return found, peak, jnp.sum(total, axis=1, keepdims=True)

    own_info = extras(side)
    frame(own_wide[:rows, :], own_framed)
    own_found, own_peak, own_total = score(own_framed, own_info)

    swap.wait()
    other_all = other_recv[...].astype(jnp.float32)
    other_info = other_all[rows : rows + part_dev, :]
    frame(other_all[:rows, :], other_framed)
    other_found, other_peak, other_total = score(other_framed, other_info)
    peak = jnp.concatenate([own_peak, other_peak], axis=0)
    total = jnp.concatenate([own_total, other_total], axis=0)
    half = lax.broadcasted_iota(jnp.int32, (group, LANES), 1) < LANES // 2
    part_send[...] = jnp.where(half, peak, total)
    share_part = pltpu.make_async_remote_copy(
        src_ref=part_send,
        dst_ref=part_recv,
        send_sem=pair_send_sem.at[1],
        recv_sem=pair_recv_sem.at[1],
        device_id={"cls": 1 - side},
        device_id_type=MESH,
    )
    share_part.start()
    by_pair = [own_info, own_info, other_info, other_info]
    ids_send[...] = jnp.concatenate(
        [
            jnp.broadcast_to(
                info[:, (2 + place % 2) * cycles : (2 + place % 2) * cycles + 1], (part_dev, LANES)
            )
            for place, info in enumerate(by_pair)
        ],
        axis=0,
    ).astype(jnp.bfloat16)
    mine = pl.ds(pl.multiple_of(me * pairs, pairs), pairs)
    ids_recv[mine, :] = ids_send[...]
    id_copies = []
    for step, peer in enumerate(peers):
        copy = pltpu.make_async_remote_copy(
            src_ref=ids_send,
            dst_ref=ids_recv.at[mine, :],
            send_sem=ids_send_sem.at[step],
            recv_sem=ids_recv_sem.at[step],
            device_id={"dom": peer},
            device_id_type=MESH,
        )
        copy.start()
        id_copies.append(copy)

    def raw_weights(found, peak):
        parts = [jnp.where(live, jnp.exp(value - peak), 0.0) for live, value in found]
        return jnp.concatenate(parts, axis=0).astype(jnp.bfloat16)

    own_raw = raw_weights(own_found, own_peak)
    other_raw = raw_weights(other_found, other_peak)
    raw_weight = jnp.concatenate(
        [jnp.sum(raw.astype(jnp.float32), axis=1, keepdims=True) for raw in (own_raw, other_raw)],
        axis=0,
    )
    filters = raw_weight * jnp.concatenate([info[:, :cycles] for info in by_pair], axis=0)
    pair_sums[:group, :] = jnp.dot(
        own_raw, own_framed[...], preferred_element_type=jnp.float32
    )
    pair_sums[group:, :] = jnp.dot(
        other_raw, other_framed[...], preferred_element_type=jnp.float32
    )
    share_part.wait()
    theirs = part_recv[...]
    theirs = jnp.concatenate([theirs[part_dev:, :], theirs[:part_dev, :]], axis=0)
    their_peak = theirs[:, :1]
    their_total = theirs[:, LANES // 2 : LANES // 2 + 1]
    top = jnp.maximum(peak, their_peak)
    both = total * jnp.exp(peak - top) + their_total * jnp.exp(their_peak - top)
    evidence = top + jnp.log(both)
    corner = lax.broadcasted_iota(jnp.int32, (group, LANES), 1) == lax.broadcasted_iota(
        jnp.int32, (group, LANES), 0
    )
    evidence_row = jnp.sum(jnp.where(corner, evidence, 0.0), axis=0, keepdims=True)
    evidence_ref[...] = evidence_row[:, :part_dev]

    scale = jnp.exp(peak - evidence)
    scale = jnp.concatenate([scale[:part_dev]] * 2 + [scale[part_dev:]] * 2, axis=0)
    filters = filters * scale

    chips = doms // 2
    chip, core = me // 2, lax.rem(me, 2)
    copies = []
    for step in [*range(1, chips), 0]:
        target = lax.rem(chip + step, chips)
        lanes = pl.ds(pl.multiple_of(target * 2 * share, LANES), 2 * share)
        terms = pair_sums[:, lanes] * scale
        for to in range(2):
            here = pl.ds(pl.multiple_of((2 * target + to) * pairs, pairs), pairs)
            stage[here, :] = jnp.concatenate(
                [terms[:, to * share : (to + 1) * share], filters], axis=1
            ).astype(jnp.bfloat16)
        for to in range(2 if step else 1):
            peer = 2 * target + to if step else me + 1 - 2 * core
            copy = pltpu.make_async_remote_copy(
                src_ref=stage.at[pl.ds(pl.multiple_of(peer * pairs, pairs), pairs), :],
                dst_ref=arrived.at[mine, :],
                send_sem=data_send_sem.at[2 * step + to],
                recv_sem=data_recv_sem.at[2 * step + core if step else 0],
                device_id={"dom": peer},
                device_id_type=MESH,
            )
            copy.start()
            copies.append((copy, 2 * step + to, peer))
    arrived[mine, :] = stage[mine, :]

    for copy in id_copies:
        copy.wait()
    ids = jnp.broadcast_to(
        ids_recv[...].astype(jnp.float32)[:, :1], (doms * pairs, class_block)
    )
    column = lax.broadcasted_iota(jnp.int32, (doms * pairs, class_block), 1).astype(jnp.float32)
    chosen_ref[...] = jnp.where(ids == column, 1.0, 0.0).astype(jnp.bfloat16)
    for copy, place, peer in copies:
        copy.wait_send()
        pltpu.make_async_remote_copy(
            src_ref=stage.at[mine, :],
            dst_ref=arrived.at[mine, :],
            send_sem=data_send_sem.at[place],
            recv_sem=data_recv_sem.at[place],
            device_id={"dom": peer},
            device_id_type=MESH,
        ).wait_recv()


def sums_kernel(arrived, chosen, evidence_in, sums_ref, weight_ref, evidence_ref):
    share = sums_ref.shape[1]
    cycles = weight_ref.shape[0]
    contract_first = (((0,), (0,)), ((), ()))
    evidence_ref[...] = evidence_in[...]
    sums = lax.dot_general(
        chosen[...], arrived[...], contract_first, preferred_element_type=jnp.float32
    )
    sums_ref[...] = sums[:, :share]
    filter_sums = lax.dot_general(
        arrived[:, share - cycles :],
        chosen[...],
        contract_first,
        preferred_element_type=jnp.float32,
    )
    weight_ref[...] = filter_sums[cycles:, :]


def paired_shards(images, ctf, inv_noise, classes, candidates):
    doms = lax.axis_size("dom")
    part_dev, features = images.shape
    cycles = ctf.shape[1]
    class_block = classes.shape[0]
    shift = features // ROTATIONS
    group = 2 * part_dev
    rows = ROTATIONS * part_dev
    pairs = TOP_CAND * group
    share = features // doms
    wide = share + cycles
    own_rows = rows + 16
    f32, bf16 = jnp.float32, jnp.bfloat16
    vmem = pl.BlockSpec(memory_space=pltpu.VMEM)
    arrived, chosen, evidence = pl.pallas_call(
        functools.partial(estep_kernel, doms),
        out_shape=(
            jax.ShapeDtypeStruct((doms * pairs, wide), bf16),
            jax.ShapeDtypeStruct((doms * pairs, class_block), bf16),
            jax.ShapeDtypeStruct((1, part_dev), f32),
        ),
        in_specs=[pl.BlockSpec(memory_space=pltpu.HBM)] * 5,
        out_specs=(vmem, vmem, vmem),
        scratch_shapes=[
            pltpu.VMEM((class_block, features), bf16),
            pltpu.VMEM((part_dev, features), bf16),
            pltpu.VMEM((part_dev, cycles), f32),
            pltpu.VMEM((1, cycles), f32),
            pltpu.VMEM((TOP_CAND, part_dev), jnp.int32),
            pltpu.VMEM((own_rows, shift), f32),
            pltpu.VMEM((own_rows, shift), bf16),
            pltpu.VMEM((own_rows, shift), bf16),
            pltpu.VMEM((4, 2 * rows, shift), bf16),
            pltpu.VMEM((rows, features), bf16),
            pltpu.VMEM((rows, features), bf16),
            pltpu.VMEM((group, LANES), f32),
            pltpu.VMEM((group, LANES), f32),
            pltpu.VMEM((pairs, LANES), bf16),
            pltpu.VMEM((doms * pairs, LANES), bf16),
            pltpu.VMEM((doms * pairs, wide), bf16),
            pltpu.VMEM((pairs, features), f32),
            pltpu.SemaphoreType.DMA((5,)),
            pltpu.SemaphoreType.DMA((2,)),
            pltpu.SemaphoreType.DMA((2,)),
            pltpu.SemaphoreType.DMA((doms - 1,)),
            pltpu.SemaphoreType.DMA((doms - 1,)),
            pltpu.SemaphoreType.DMA((doms,)),
            pltpu.SemaphoreType.DMA((doms,)),
        ],
        compiler_params=pltpu.CompilerParams(
            collective_id=0, has_side_effects=True, vmem_limit_bytes=63 * 1024 * 1024
        ),
    )(images, ctf, inv_noise[None, :], candidates.T, classes)
    sums, weight, evidence = pl.pallas_call(
        sums_kernel,
        out_shape=(
            jax.ShapeDtypeStruct((class_block, share), f32),
            jax.ShapeDtypeStruct((cycles, class_block), f32),
            jax.ShapeDtypeStruct((1, part_dev), f32),
        ),
        in_specs=[vmem] * 3,
        out_specs=(vmem, vmem, vmem),
        compiler_params=pltpu.CompilerParams(vmem_limit_bytes=63 * 1024 * 1024),
    )(arrived, chosen, evidence)
    return sums.T, weight.T, evidence.reshape(part_dev)


def pick_plan(images, ctf, inv_noise, classes, candidates):
    doms = lax.axis_size("dom")
    part_dev, features = images.shape
    cycles = ctf.shape[1]
    fits = (
        lax.axis_size("cls") == 2
        and part_dev == 4
        and 2 * cycles == LANES
        and features == ROTATIONS * 2 * LANES
        and doms % 2 == 0
        and (features // doms) % LANES == cycles
        and classes.shape[0] <= 256
    )
    plan = paired_shards if fits else shards
    return plan(images, ctf, inv_noise, classes, candidates)


def solution(mesh):
    in_specs = (
        P(("dom", "cls"), None),
        P(("dom", "cls"), None),
        P(),
        P("cls", None),
        P(("dom", "cls"), None),
    )
    out_specs = (P("dom", "cls"), P("cls", None), P(("dom", "cls")))
    return jax.shard_map(
        pick_plan, mesh=mesh, in_specs=in_specs, out_specs=out_specs, check_vma=False
    )
```

```python
import functools
import math

import jax
import jax.numpy as jnp
from jax import lax
from jax.experimental import pallas as pl
from jax.experimental.pallas import tpu as pltpu
from jax.sharding import PartitionSpec as P

ANGLES = 72
ROTATIONS = 36
TOP_CAND = 2


NEGATIVE = -1e30


def combined_all(value, axis, join):
    pieces = jax.tree.map(lambda part: lax.all_gather(part, axis), value)
    head = jax.tree.map(lambda part: part[0], pieces)
    tail = jax.tree.map(lambda part: part[1:], pieces)
    subtotal, _ = lax.scan(lambda subtotal, section: (join(subtotal, section), None), head, tail)
    return subtotal


def combine_totals(earlier, later):
    highest = jnp.maximum(earlier[0], later[0])
    return (
        highest,
        earlier[1] * jnp.exp(earlier[0] - highest) + later[1] * jnp.exp(later[0] - highest),
    )


def shards(images, ctf, inv_noise, classes, candidates):
    cls_count = lax.axis_size("cls")
    my_index = lax.axis_index("cls")
    part_dev = images.shape[0]
    class_block = classes.shape[0]
    features = images.shape[1]
    cycles = ctf.shape[1]
    capacity = min(5 * part_dev * TOP_CAND // (2 * cls_count), part_dev)
    group_size = cls_count * part_dev
    shift = features // ANGLES * (ANGLES // ROTATIONS)
    turn_ids = jnp.arange(ROTATIONS, dtype=jnp.int32)
    ctf_noise = ctf * inv_noise[None, :]
    weighted = (images.astype(jnp.float32) * jnp.tile(ctf_noise, (1, features // cycles))).astype(
        jnp.bfloat16
    )
    quadratic = (ctf * ctf * inv_noise[None, :]).astype(jnp.bfloat16)
    everyone = lax.all_gather(candidates, "cls", axis=0, tiled=True)
    block_ids = jnp.arange(class_block, dtype=jnp.int32) + my_index * class_block
    cand_mask = jnp.any(everyone[:, :, None] == block_ids[None, None, :], axis=1).astype(
        jnp.float32
    )
    owner_ids = jnp.arange(cls_count, dtype=jnp.int32)
    routed = jnp.any(
        (everyone // class_block)[:, :, None] == owner_ids[None, None, :], axis=1
    ).astype(jnp.int32)
    by_source = routed.reshape(cls_count, part_dev, cls_count)
    slot_of = jnp.cumsum(by_source, axis=1) - by_source
    slot_ids = jnp.arange(capacity, dtype=jnp.int32)
    mine_routed = lax.dynamic_index_in_dim(by_source, my_index, 0, keepdims=False)
    mine_slot = lax.dynamic_index_in_dim(slot_of, my_index, 0, keepdims=False)
    packing = (mine_routed.T[:, None, :] == 1) & (
        mine_slot.T[:, None, :] == slot_ids[None, :, None]
    )
    packing = packing.reshape(cls_count * capacity, part_dev).astype(jnp.bfloat16)
    send_data = jnp.dot(packing, weighted, preferred_element_type=jnp.float32).astype(jnp.bfloat16)
    send_quad = jnp.dot(packing, quadratic, preferred_element_type=jnp.float32).astype(jnp.bfloat16)
    row_data, row_quad = (
        lax.all_to_all(send_data, "cls", split_axis=0, concat_axis=0, tiled=True),
        lax.all_to_all(send_quad, "cls", split_axis=0, concat_axis=0, tiled=True),
    )
    into_mine = lax.dynamic_index_in_dim(by_source, my_index, 2, keepdims=False)
    slot_mine = lax.dynamic_index_in_dim(slot_of, my_index, 2, keepdims=False)
    selected = (into_mine[:, None, :] == 1) & (slot_mine[:, None, :] == slot_ids[None, :, None])
    diagonal = jnp.eye(cls_count, dtype=jnp.float32)
    unpack = (selected.astype(jnp.float32)[:, :, None, :] * diagonal[:, None, :, None]).reshape(
        cls_count * capacity, group_size
    )
    row_mask = jnp.dot(unpack, cand_mask, precision=lax.Precision.HIGHEST)
    row_count = row_data.shape[0]
    energy = jnp.sum(
        jnp.square(classes.astype(jnp.float32)).reshape(class_block, features // cycles, cycles),
        axis=1,
    )
    quad_wide = row_quad.astype(jnp.float32)
    norm_term = jnp.dot(quad_wide, energy.T, precision=lax.Precision.HIGHEST)
    twin_classes = jnp.concatenate([classes, classes], axis=1)
    feat_block = math.gcd(features, 1152)

    def add_block(block_index, running):
        offset = block_index * feat_block
        rotated = jax.vmap(
            lambda rotation: lax.dynamic_slice_in_dim(
                twin_classes, offset - rotation * shift + features, feat_block, 1
            )
        )(turn_ids)
        section = lax.dynamic_slice_in_dim(row_data, offset, feat_block, 1)
        return running + lax.dot_general(
            section, rotated, (((1,), (2,)), ((), ())), preferred_element_type=jnp.float32
        )

    cross = lax.fori_loop(
        0,
        features // feat_block,
        add_block,
        jnp.zeros((row_count, ROTATIONS, class_block), jnp.float32),
    )
    logits = cross - 0.5 * norm_term[:, None, :]
    live = jnp.broadcast_to(row_mask[:, None, :] > 0.5, logits.shape)
    masked = jnp.where(live, logits, NEGATIVE)
    peak = jnp.max(masked, axis=(1, 2))
    part_total = jnp.sum(jnp.where(live, jnp.exp(masked - peak[:, None, None]), 0.0), axis=(1, 2))
    group_peak = jnp.max(jnp.where(unpack > 0.5, peak[:, None], NEGATIVE), axis=0)
    group_total = jnp.sum(unpack * part_total[:, None], axis=0)
    top_all, total_all = combined_all((group_peak, group_total), "cls", combine_totals)
    group_evidence = top_all + jnp.log(total_all)
    own_evidence = lax.dynamic_slice_in_dim(group_evidence, my_index * part_dev, part_dev, 0)
    row_evidence = jnp.dot(unpack, group_evidence, precision=lax.Precision.HIGHEST)
    posterior = jnp.where(live, jnp.exp(logits - row_evidence[:, None, None]), 0.0).astype(
        jnp.bfloat16
    )
    weight_total = jnp.sum(posterior.astype(jnp.float32), axis=1)
    ctf_part = jnp.dot(weight_total.T, quad_wide, precision=lax.Precision.HIGHEST)
    weight_sums = lax.psum(ctf_part, "dom")
    twin_rows = jnp.concatenate([row_data, row_data], axis=1)

    def add_sums(block_index, running):
        offset = block_index * feat_block
        stacked = jax.vmap(
            lambda rotation: lax.dynamic_slice_in_dim(
                twin_rows, offset + rotation * shift, feat_block, 1
            )
        )(turn_ids)
        block_sum = lax.dot_general(
            posterior, stacked, (((0, 1), (1, 0)), ((), ())), preferred_element_type=jnp.float32
        )
        return lax.dynamic_update_slice_in_dim(running, block_sum, offset, 1)

    summed = lax.fori_loop(
        0, features // feat_block, add_sums, jnp.zeros((class_block, features), jnp.float32)
    )
    full_term = summed.T
    class_sums = lax.psum_scatter(full_term, "dom", scatter_dimension=0, tiled=True)
    return (class_sums, weight_sums, own_evidence)


MESH = pl.DeviceIdType.MESH
LANES = 128


def estep_kernel(
    doms,
    images_ref,
    ctf_ref,
    noise_ref,
    cand_ref,
    classes_ref,
    arrived,
    evidence_ref,
    held,
    images_vmem,
    ctf_vmem,
    noise_vmem,
    cand_vmem,
    own_wide,
    own_send,
    other_recv,
    twins,
    own_framed,
    other_framed,
    part_send,
    part_recv,
    stage,
    pair_sums,
    load_sem,
    pair_send_sem,
    pair_recv_sem,
    data_send_sem,
    data_recv_sem,
):
    me = lax.axis_index("dom")
    side = lax.axis_index("cls")
    part_dev, features = images_ref.shape
    cycles = ctf_ref.shape[1]
    class_block = held.shape[0]
    shift = features // ROTATIONS
    group = 2 * part_dev
    pairs = TOP_CAND * group
    rows = ROTATIONS * part_dev
    share = features // doms
    wide = stage.shape[1]
    peers = [lax.rem(me + step, doms) for step in range(1, doms)]

    loads = [
        pltpu.make_async_copy(source, target, load_sem.at[place])
        for place, (source, target) in enumerate(
            [
                (cand_ref, cand_vmem),
                (noise_ref, noise_vmem),
                (ctf_ref, ctf_vmem),
                (images_ref, images_vmem),
                (classes_ref, held),
            ]
        )
    ]
    for load in loads:
        load.start()
    barrier = pltpu.get_barrier_semaphore()
    pl.semaphore_signal(barrier, inc=1, device_id={"cls": 1 - side}, device_id_type=MESH)
    for peer in peers:
        pl.semaphore_signal(barrier, inc=1, device_id={"dom": peer}, device_id_type=MESH)

    for load in loads[:4]:
        load.wait()
    ctf = ctf_vmem[...]
    noise = noise_vmem[...]
    factor = jnp.concatenate([ctf * noise] * (shift // cycles), axis=1)
    quad = (ctf * ctf * noise).astype(jnp.bfloat16).astype(jnp.float32)
    cand = cand_vmem[...].astype(jnp.float32)
    square = (part_dev, part_dev)
    same = lax.broadcasted_iota(jnp.int32, square, 0) == lax.broadcasted_iota(jnp.int32, square, 1)

    def local_ids(block, column):
        ids = jnp.broadcast_to(cand[column : column + 1, :], square)
        ids = jnp.sum(jnp.where(same, ids, 0.0), axis=1, keepdims=True)
        local = ids - (block * class_block).astype(jnp.float32)
        inside = (local >= 0.0) & (local < class_block)
        return jnp.broadcast_to(jnp.where(inside, local, -1.0), (part_dev, cycles))

    def extras(block):
        return jnp.concatenate([quad, quad, local_ids(block, 0), local_ids(block, 1)], axis=1)

    for turn in range(ROTATIONS):
        piece = images_vmem[:, turn * shift : (turn + 1) * shift].astype(jnp.float32) * factor
        piece = piece.astype(jnp.bfloat16).astype(jnp.float32)
        own_wide[turn * part_dev : (turn + 1) * part_dev, :] = piece
    own_wide[rows : rows + 16, :] = jnp.zeros((16, shift), jnp.float32)
    own_wide[rows : rows + part_dev, :] = extras(1 - side)
    own_send[...] = own_wide[...].astype(jnp.bfloat16)

    pl.semaphore_wait(barrier, doms)
    swap = pltpu.make_async_remote_copy(
        src_ref=own_send,
        dst_ref=other_recv,
        send_sem=pair_send_sem.at[0],
        recv_sem=pair_recv_sem.at[0],
        device_id={"cls": 1 - side},
        device_id_type=MESH,
    )
    swap.start()

    loads[4].wait()
    energy = jnp.zeros((class_block, LANES), jnp.float32)
    for start in range(0, features, LANES):
        part = held[:, start : start + LANES].astype(jnp.float32)
        energy = energy + part * part

    def frame(values, framed):
        doubled = jnp.concatenate([values, values], axis=0)
        for late in range(4):
            cut = late * part_dev
            moved = jnp.concatenate([doubled[cut:], doubled[:cut]], axis=0) if cut else doubled
            twins[late] = moved.astype(jnp.bfloat16)
        for turn in range(ROTATIONS):
            begin = turn // 4 * 4 * part_dev
            framed[:, turn * shift : (turn + 1) * shift] = twins[turn % 4, begin : begin + rows, :]

    contract_last = (((1,), (1,)), ((), ()))
    lane = lax.broadcasted_iota(jnp.int32, (part_dev, rows), 1)
    own_lane = (lane & (part_dev - 1)) == lax.broadcasted_iota(jnp.int32, (part_dev, rows), 0)
    class_row = lax.broadcasted_iota(jnp.int32, (class_block, rows), 0).astype(jnp.float32)

    def score(framed, info):
        cross = lax.dot_general(
            held[...], framed[...], contract_last, preferred_element_type=jnp.float32
        )
        norm = lax.dot_general(
            energy,
            jnp.concatenate([info[:, :LANES]] * ROTATIONS, axis=0),
            contract_last,
            precision=lax.Precision.HIGHEST,
            preferred_element_type=jnp.float32,
        )
        logits = cross - 0.5 * norm
        found = []
        for place in range(TOP_CAND):
            ids = info[:, (2 + place) * cycles : (2 + place) * cycles + 1]
            wanted = jnp.sum(jnp.where(own_lane, ids, 0.0), axis=0, keepdims=True)
            value = jnp.sum(jnp.where(class_row == wanted, logits, 0.0), axis=0, keepdims=True)
            live = own_lane & (ids >= 0.0)
            found.append((live, jnp.where(live, value, NEGATIVE)))
        peak = functools.reduce(jnp.maximum, [value for live, value in found])
        peak = jnp.max(peak, axis=1, keepdims=True)
        total = sum(jnp.where(live, jnp.exp(value - peak), 0.0) for live, value in found)
        return found, peak, jnp.sum(total, axis=1, keepdims=True)

    own_info = extras(side)
    frame(own_wide[:rows, :], own_framed)
    own_found, own_peak, own_total = score(own_framed, own_info)

    swap.wait()
    other_all = other_recv[...].astype(jnp.float32)
    other_info = other_all[rows : rows + part_dev, :]
    frame(other_all[:rows, :], other_framed)
    other_found, other_peak, other_total = score(other_framed, other_info)
    peak = jnp.concatenate([own_peak, other_peak], axis=0)
    total = jnp.concatenate([own_total, other_total], axis=0)
    half = lax.broadcasted_iota(jnp.int32, (group, LANES), 1) < LANES // 2
    part_send[...] = jnp.where(half, peak, total)
    share_part = pltpu.make_async_remote_copy(
        src_ref=part_send,
        dst_ref=part_recv,
        send_sem=pair_send_sem.at[1],
        recv_sem=pair_recv_sem.at[1],
        device_id={"cls": 1 - side},
        device_id_type=MESH,
    )
    share_part.start()
    by_pair = [own_info, own_info, other_info, other_info]
    pair_ids = jnp.concatenate(
        [
            jnp.broadcast_to(
                info[:, (2 + place % 2) * cycles : (2 + place % 2) * cycles + 1], (part_dev, LANES)
            )
            for place, info in enumerate(by_pair)
        ],
        axis=0,
    )
    mine = pl.ds(pl.multiple_of(me * pairs, pairs), pairs)
    def raw_weights(found, peak):
        parts = [jnp.where(live, jnp.exp(value - peak), 0.0) for live, value in found]
        return jnp.concatenate(parts, axis=0).astype(jnp.bfloat16)

    own_raw = raw_weights(own_found, own_peak)
    other_raw = raw_weights(other_found, other_peak)
    raw_weight = jnp.concatenate(
        [jnp.sum(raw.astype(jnp.float32), axis=1, keepdims=True) for raw in (own_raw, other_raw)],
        axis=0,
    )
    filters = raw_weight * jnp.concatenate([info[:, :cycles] for info in by_pair], axis=0)
    pair_sums[:group, :] = jnp.dot(
        own_raw, own_framed[...], preferred_element_type=jnp.float32
    )
    pair_sums[group:, :] = jnp.dot(
        other_raw, other_framed[...], preferred_element_type=jnp.float32
    )
    share_part.wait()
    theirs = part_recv[...]
    theirs = jnp.concatenate([theirs[part_dev:, :], theirs[:part_dev, :]], axis=0)
    their_peak = theirs[:, :1]
    their_total = theirs[:, LANES // 2 : LANES // 2 + 1]
    top = jnp.maximum(peak, their_peak)
    both = total * jnp.exp(peak - top) + their_total * jnp.exp(their_peak - top)
    evidence = top + jnp.log(both)
    corner = lax.broadcasted_iota(jnp.int32, (group, LANES), 1) == lax.broadcasted_iota(
        jnp.int32, (group, LANES), 0
    )
    evidence_row = jnp.sum(jnp.where(corner, evidence, 0.0), axis=0, keepdims=True)
    evidence_ref[...] = evidence_row[:, :part_dev]

    scale = jnp.exp(peak - evidence)
    scale = jnp.concatenate([scale[:part_dev]] * 2 + [scale[part_dev:]] * 2, axis=0)
    filters = filters * scale

    chips = doms // 2
    chip, core = me // 2, lax.rem(me, 2)
    copies = []
    for step in [*range(1, chips), 0]:
        target = lax.rem(chip + step, chips)
        lanes = pl.ds(pl.multiple_of(target * 2 * share, LANES), 2 * share)
        terms = pair_sums[:, lanes] * scale
        for to in range(2):
            here = pl.ds(pl.multiple_of((2 * target + to) * pairs, pairs), pairs)
            stage[here, :] = jnp.concatenate(
                [terms[:, to * share : (to + 1) * share], filters, pair_ids], axis=1
            ).astype(jnp.bfloat16)
        for to in range(2 if step else 1):
            peer = 2 * target + to if step else me + 1 - 2 * core
            copy = pltpu.make_async_remote_copy(
                src_ref=stage.at[pl.ds(pl.multiple_of(peer * pairs, pairs), pairs), :],
                dst_ref=arrived.at[mine, :],
                send_sem=data_send_sem.at[2 * step + to],
                recv_sem=data_recv_sem.at[2 * step + core if step else 0],
                device_id={"dom": peer},
                device_id_type=MESH,
            )
            copy.start()
            copies.append((copy, 2 * step + to, peer))
    arrived[mine, :] = stage[mine, :]

    for copy, place, peer in copies:
        copy.wait_send()
        pltpu.make_async_remote_copy(
            src_ref=stage.at[mine, :],
            dst_ref=arrived.at[mine, :],
            send_sem=data_send_sem.at[place],
            recv_sem=data_recv_sem.at[place],
            device_id={"dom": peer},
            device_id_type=MESH,
        ).wait_recv()


def sums_kernel(arrived, evidence_in, sums_ref, weight_ref, evidence_ref):
    share = sums_ref.shape[1]
    cycles = weight_ref.shape[0]
    contract_first = (((0,), (0,)), ((), ()))
    evidence_ref[...] = evidence_in[...]
    block = (arrived.shape[0], sums_ref.shape[0])
    ids = arrived[:, share + cycles :].astype(jnp.float32)[:, :1]
    column = lax.broadcasted_iota(jnp.int32, block, 1).astype(jnp.float32)
    chosen = jnp.where(jnp.broadcast_to(ids, block) == column, 1.0, 0.0).astype(jnp.bfloat16)
    sums = lax.dot_general(
        chosen, arrived[:, : share + cycles], contract_first, preferred_element_type=jnp.float32
    )
    sums_ref[...] = sums[:, :share]
    filter_sums = lax.dot_general(
        arrived[:, share - cycles : share + cycles],
        chosen,
        contract_first,
        preferred_element_type=jnp.float32,
    )
    weight_ref[...] = filter_sums[cycles:, :]


def paired_shards(images, ctf, inv_noise, classes, candidates):
    doms = lax.axis_size("dom")
    part_dev, features = images.shape
    cycles = ctf.shape[1]
    class_block = classes.shape[0]
    shift = features // ROTATIONS
    group = 2 * part_dev
    rows = ROTATIONS * part_dev
    pairs = TOP_CAND * group
    share = features // doms
    wide = share + cycles + LANES
    own_rows = rows + 16
    f32, bf16 = jnp.float32, jnp.bfloat16
    vmem = pl.BlockSpec(memory_space=pltpu.VMEM)
    arrived, evidence = pl.pallas_call(
        functools.partial(estep_kernel, doms),
        out_shape=(
            jax.ShapeDtypeStruct((doms * pairs, wide), bf16),
            jax.ShapeDtypeStruct((1, part_dev), f32),
        ),
        in_specs=[pl.BlockSpec(memory_space=pltpu.HBM)] * 5,
        out_specs=(vmem, vmem),
        scratch_shapes=[
            pltpu.VMEM((class_block, features), bf16),
            pltpu.VMEM((part_dev, features), bf16),
            pltpu.VMEM((part_dev, cycles), f32),
            pltpu.VMEM((1, cycles), f32),
            pltpu.VMEM((TOP_CAND, part_dev), jnp.int32),
            pltpu.VMEM((own_rows, shift), f32),
            pltpu.VMEM((own_rows, shift), bf16),
            pltpu.VMEM((own_rows, shift), bf16),
            pltpu.VMEM((4, 2 * rows, shift), bf16),
            pltpu.VMEM((rows, features), bf16),
            pltpu.VMEM((rows, features), bf16),
            pltpu.VMEM((group, LANES), f32),
            pltpu.VMEM((group, LANES), f32),
            pltpu.VMEM((doms * pairs, wide), bf16),
            pltpu.VMEM((pairs, features), f32),
            pltpu.SemaphoreType.DMA((5,)),
            pltpu.SemaphoreType.DMA((2,)),
            pltpu.SemaphoreType.DMA((2,)),
            pltpu.SemaphoreType.DMA((doms,)),
            pltpu.SemaphoreType.DMA((doms,)),
        ],
        compiler_params=pltpu.CompilerParams(
            collective_id=0, has_side_effects=True, vmem_limit_bytes=63 * 1024 * 1024
        ),
    )(images, ctf, inv_noise[None, :], candidates.T, classes)
    sums, weight, evidence = pl.pallas_call(
        sums_kernel,
        out_shape=(
            jax.ShapeDtypeStruct((class_block, share), f32),
            jax.ShapeDtypeStruct((cycles, class_block), f32),
            jax.ShapeDtypeStruct((1, part_dev), f32),
        ),
        in_specs=[vmem] * 2,
        out_specs=(vmem, vmem, vmem),
        compiler_params=pltpu.CompilerParams(vmem_limit_bytes=63 * 1024 * 1024),
    )(arrived, evidence)
    return sums.T, weight.T, evidence.reshape(part_dev)


def pick_plan(images, ctf, inv_noise, classes, candidates):
    doms = lax.axis_size("dom")
    part_dev, features = images.shape
    cycles = ctf.shape[1]
    fits = (
        lax.axis_size("cls") == 2
        and part_dev == 4
        and 2 * cycles == LANES
        and features == ROTATIONS * 2 * LANES
        and doms % 2 == 0
        and (features // doms) % LANES == cycles
        and classes.shape[0] <= 256
    )
    plan = paired_shards if fits else shards
    return plan(images, ctf, inv_noise, classes, candidates)


def solution(mesh):
    in_specs = (
        P(("dom", "cls"), None),
        P(("dom", "cls"), None),
        P(),
        P("cls", None),
        P(("dom", "cls"), None),
    )
    out_specs = (P("dom", "cls"), P("cls", None), P(("dom", "cls")))
    return jax.shard_map(
        pick_plan, mesh=mesh, in_specs=in_specs, out_specs=out_specs, check_vma=False
    )
```

```python
import functools
import math

import jax
import jax.numpy as jnp
from jax import lax
from jax.experimental import pallas as pl
from jax.experimental.pallas import tpu as pltpu
from jax.sharding import PartitionSpec as P

ANGLES = 72
ROTATIONS = 36
TOP_CAND = 2


NEGATIVE = -1e30


def combined_all(value, axis, join):
    pieces = jax.tree.map(lambda part: lax.all_gather(part, axis), value)
    head = jax.tree.map(lambda part: part[0], pieces)
    tail = jax.tree.map(lambda part: part[1:], pieces)
    subtotal, _ = lax.scan(lambda subtotal, section: (join(subtotal, section), None), head, tail)
    return subtotal


def combine_totals(earlier, later):
    highest = jnp.maximum(earlier[0], later[0])
    return (
        highest,
        earlier[1] * jnp.exp(earlier[0] - highest) + later[1] * jnp.exp(later[0] - highest),
    )


def shards(images, ctf, inv_noise, classes, candidates):
    cls_count = lax.axis_size("cls")
    my_index = lax.axis_index("cls")
    part_dev = images.shape[0]
    class_block = classes.shape[0]
    features = images.shape[1]
    cycles = ctf.shape[1]
    capacity = min(5 * part_dev * TOP_CAND // (2 * cls_count), part_dev)
    group_size = cls_count * part_dev
    shift = features // ANGLES * (ANGLES // ROTATIONS)
    turn_ids = jnp.arange(ROTATIONS, dtype=jnp.int32)
    ctf_noise = ctf * inv_noise[None, :]
    weighted = (images.astype(jnp.float32) * jnp.tile(ctf_noise, (1, features // cycles))).astype(
        jnp.bfloat16
    )
    quadratic = (ctf * ctf * inv_noise[None, :]).astype(jnp.bfloat16)
    everyone = lax.all_gather(candidates, "cls", axis=0, tiled=True)
    block_ids = jnp.arange(class_block, dtype=jnp.int32) + my_index * class_block
    cand_mask = jnp.any(everyone[:, :, None] == block_ids[None, None, :], axis=1).astype(
        jnp.float32
    )
    owner_ids = jnp.arange(cls_count, dtype=jnp.int32)
    routed = jnp.any(
        (everyone // class_block)[:, :, None] == owner_ids[None, None, :], axis=1
    ).astype(jnp.int32)
    by_source = routed.reshape(cls_count, part_dev, cls_count)
    slot_of = jnp.cumsum(by_source, axis=1) - by_source
    slot_ids = jnp.arange(capacity, dtype=jnp.int32)
    mine_routed = lax.dynamic_index_in_dim(by_source, my_index, 0, keepdims=False)
    mine_slot = lax.dynamic_index_in_dim(slot_of, my_index, 0, keepdims=False)
    packing = (mine_routed.T[:, None, :] == 1) & (
        mine_slot.T[:, None, :] == slot_ids[None, :, None]
    )
    packing = packing.reshape(cls_count * capacity, part_dev).astype(jnp.bfloat16)
    send_data = jnp.dot(packing, weighted, preferred_element_type=jnp.float32).astype(jnp.bfloat16)
    send_quad = jnp.dot(packing, quadratic, preferred_element_type=jnp.float32).astype(jnp.bfloat16)
    row_data, row_quad = (
        lax.all_to_all(send_data, "cls", split_axis=0, concat_axis=0, tiled=True),
        lax.all_to_all(send_quad, "cls", split_axis=0, concat_axis=0, tiled=True),
    )
    into_mine = lax.dynamic_index_in_dim(by_source, my_index, 2, keepdims=False)
    slot_mine = lax.dynamic_index_in_dim(slot_of, my_index, 2, keepdims=False)
    selected = (into_mine[:, None, :] == 1) & (slot_mine[:, None, :] == slot_ids[None, :, None])
    diagonal = jnp.eye(cls_count, dtype=jnp.float32)
    unpack = (selected.astype(jnp.float32)[:, :, None, :] * diagonal[:, None, :, None]).reshape(
        cls_count * capacity, group_size
    )
    row_mask = jnp.dot(unpack, cand_mask, precision=lax.Precision.HIGHEST)
    row_count = row_data.shape[0]
    energy = jnp.sum(
        jnp.square(classes.astype(jnp.float32)).reshape(class_block, features // cycles, cycles),
        axis=1,
    )
    quad_wide = row_quad.astype(jnp.float32)
    norm_term = jnp.dot(quad_wide, energy.T, precision=lax.Precision.HIGHEST)
    twin_classes = jnp.concatenate([classes, classes], axis=1)
    feat_block = math.gcd(features, 1152)

    def add_block(block_index, running):
        offset = block_index * feat_block
        rotated = jax.vmap(
            lambda rotation: lax.dynamic_slice_in_dim(
                twin_classes, offset - rotation * shift + features, feat_block, 1
            )
        )(turn_ids)
        section = lax.dynamic_slice_in_dim(row_data, offset, feat_block, 1)
        return running + lax.dot_general(
            section, rotated, (((1,), (2,)), ((), ())), preferred_element_type=jnp.float32
        )

    cross = lax.fori_loop(
        0,
        features // feat_block,
        add_block,
        jnp.zeros((row_count, ROTATIONS, class_block), jnp.float32),
    )
    logits = cross - 0.5 * norm_term[:, None, :]
    live = jnp.broadcast_to(row_mask[:, None, :] > 0.5, logits.shape)
    masked = jnp.where(live, logits, NEGATIVE)
    peak = jnp.max(masked, axis=(1, 2))
    part_total = jnp.sum(jnp.where(live, jnp.exp(masked - peak[:, None, None]), 0.0), axis=(1, 2))
    group_peak = jnp.max(jnp.where(unpack > 0.5, peak[:, None], NEGATIVE), axis=0)
    group_total = jnp.sum(unpack * part_total[:, None], axis=0)
    top_all, total_all = combined_all((group_peak, group_total), "cls", combine_totals)
    group_evidence = top_all + jnp.log(total_all)
    own_evidence = lax.dynamic_slice_in_dim(group_evidence, my_index * part_dev, part_dev, 0)
    row_evidence = jnp.dot(unpack, group_evidence, precision=lax.Precision.HIGHEST)
    posterior = jnp.where(live, jnp.exp(logits - row_evidence[:, None, None]), 0.0).astype(
        jnp.bfloat16
    )
    weight_total = jnp.sum(posterior.astype(jnp.float32), axis=1)
    ctf_part = jnp.dot(weight_total.T, quad_wide, precision=lax.Precision.HIGHEST)
    weight_sums = lax.psum(ctf_part, "dom")
    twin_rows = jnp.concatenate([row_data, row_data], axis=1)

    def add_sums(block_index, running):
        offset = block_index * feat_block
        stacked = jax.vmap(
            lambda rotation: lax.dynamic_slice_in_dim(
                twin_rows, offset + rotation * shift, feat_block, 1
            )
        )(turn_ids)
        block_sum = lax.dot_general(
            posterior, stacked, (((0, 1), (1, 0)), ((), ())), preferred_element_type=jnp.float32
        )
        return lax.dynamic_update_slice_in_dim(running, block_sum, offset, 1)

    summed = lax.fori_loop(
        0, features // feat_block, add_sums, jnp.zeros((class_block, features), jnp.float32)
    )
    full_term = summed.T
    class_sums = lax.psum_scatter(full_term, "dom", scatter_dimension=0, tiled=True)
    return (class_sums, weight_sums, own_evidence)


MESH = pl.DeviceIdType.MESH
LANES = 128


def estep_kernel(
    doms,
    images_ref,
    ctf_ref,
    noise_ref,
    cand_ref,
    classes_ref,
    arrived,
    chosen_ref,
    evidence_ref,
    held,
    images_vmem,
    ctf_vmem,
    noise_vmem,
    cand_vmem,
    own_wide,
    own_send,
    other_recv,
    twins,
    own_framed,
    other_framed,
    part_send,
    part_recv,
    ids_send,
    ids_recv,
    stage,
    pair_sums,
    load_sem,
    pair_send_sem,
    pair_recv_sem,
    ids_send_sem,
    ids_recv_sem,
    data_send_sem,
    data_recv_sem,
):
    me = lax.axis_index("dom")
    side = lax.axis_index("cls")
    part_dev, features = images_ref.shape
    cycles = ctf_ref.shape[1]
    class_block = held.shape[0]
    shift = features // ROTATIONS
    group = 2 * part_dev
    pairs = TOP_CAND * group
    rows = ROTATIONS * part_dev
    share = features // doms
    wide = stage.shape[1]
    peers = [lax.rem(me + step, doms) for step in range(1, doms)]

    loads = [
        pltpu.make_async_copy(source, target, load_sem.at[place])
        for place, (source, target) in enumerate(
            [
                (cand_ref, cand_vmem),
                (noise_ref, noise_vmem),
                (ctf_ref, ctf_vmem),
                (images_ref, images_vmem),
                (classes_ref, held),
            ]
        )
    ]
    for load in loads:
        load.start()
    barrier = pltpu.get_barrier_semaphore()
    pl.semaphore_signal(barrier, inc=1, device_id={"cls": 1 - side}, device_id_type=MESH)
    for peer in peers:
        pl.semaphore_signal(barrier, inc=1, device_id={"dom": peer}, device_id_type=MESH)

    for load in loads[:4]:
        load.wait()
    ctf = ctf_vmem[...]
    noise = noise_vmem[...]
    factor = jnp.concatenate([ctf * noise] * (shift // cycles), axis=1)
    quad = (ctf * ctf * noise).astype(jnp.bfloat16).astype(jnp.float32)
    cand = cand_vmem[...].astype(jnp.float32)
    square = (part_dev, part_dev)
    same = lax.broadcasted_iota(jnp.int32, square, 0) == lax.broadcasted_iota(jnp.int32, square, 1)

    def local_ids(block, column):
        ids = jnp.broadcast_to(cand[column : column + 1, :], square)
        ids = jnp.sum(jnp.where(same, ids, 0.0), axis=1, keepdims=True)
        local = ids - (block * class_block).astype(jnp.float32)
        inside = (local >= 0.0) & (local < class_block)
        return jnp.broadcast_to(jnp.where(inside, local, -1.0), (part_dev, cycles))

    def extras(block):
        return jnp.concatenate([quad, quad, local_ids(block, 0), local_ids(block, 1)], axis=1)

    for turn in range(ROTATIONS):
        piece = images_vmem[:, turn * shift : (turn + 1) * shift].astype(jnp.float32) * factor
        piece = piece.astype(jnp.bfloat16).astype(jnp.float32)
        own_wide[turn * part_dev : (turn + 1) * part_dev, :] = piece
    own_wide[rows : rows + 16, :] = jnp.zeros((16, shift), jnp.float32)
    own_wide[rows : rows + part_dev, :] = extras(1 - side)
    own_send[...] = own_wide[...].astype(jnp.bfloat16)

    pl.semaphore_wait(barrier, doms)
    swap = pltpu.make_async_remote_copy(
        src_ref=own_send,
        dst_ref=other_recv,
        send_sem=pair_send_sem.at[0],
        recv_sem=pair_recv_sem.at[0],
        device_id={"cls": 1 - side},
        device_id_type=MESH,
    )
    swap.start()

    loads[4].wait()
    energy = jnp.zeros((class_block, LANES), jnp.float32)
    for start in range(0, features, LANES):
        part = held[:, start : start + LANES].astype(jnp.float32)
        energy = energy + part * part

    def frame(values, framed):
        doubled = jnp.concatenate([values, values], axis=0)
        for late in range(4):
            cut = late * part_dev
            moved = jnp.concatenate([doubled[cut:], doubled[:cut]], axis=0) if cut else doubled
            twins[late] = moved.astype(jnp.bfloat16)
        for turn in range(ROTATIONS):
            begin = turn // 4 * 4 * part_dev
            framed[:, turn * shift : (turn + 1) * shift] = twins[turn % 4, begin : begin + rows, :]

    contract_last = (((1,), (1,)), ((), ()))
    lane = lax.broadcasted_iota(jnp.int32, (part_dev, rows), 1)
    own_lane = (lane & (part_dev - 1)) == lax.broadcasted_iota(jnp.int32, (part_dev, rows), 0)
    class_row = lax.broadcasted_iota(jnp.int32, (class_block, rows), 0).astype(jnp.float32)

    def score(framed, info):
        cross = lax.dot_general(
            held[...], framed[...], contract_last, preferred_element_type=jnp.float32
        )
        norm = lax.dot_general(
            energy,
            jnp.concatenate([info[:, :LANES]] * ROTATIONS, axis=0),
            contract_last,
            precision=lax.Precision.HIGHEST,
            preferred_element_type=jnp.float32,
        )
        logits = cross - 0.5 * norm
        found = []
        for place in range(TOP_CAND):
            ids = info[:, (2 + place) * cycles : (2 + place) * cycles + 1]
            wanted = jnp.sum(jnp.where(own_lane, ids, 0.0), axis=0, keepdims=True)
            value = jnp.sum(jnp.where(class_row == wanted, logits, 0.0), axis=0, keepdims=True)
            live = own_lane & (ids >= 0.0)
            found.append((live, jnp.where(live, value, NEGATIVE)))
        peak = functools.reduce(jnp.maximum, [value for live, value in found])
        peak = jnp.max(peak, axis=1, keepdims=True)
        total = sum(jnp.where(live, jnp.exp(value - peak), 0.0) for live, value in found)
        return found, peak, jnp.sum(total, axis=1, keepdims=True)

    own_info = extras(side)
    frame(own_wide[:rows, :], own_framed)
    own_found, own_peak, own_total = score(own_framed, own_info)

    swap.wait()
    other_all = other_recv[...].astype(jnp.float32)
    other_info = other_all[rows : rows + part_dev, :]
    frame(other_all[:rows, :], other_framed)
    other_found, other_peak, other_total = score(other_framed, other_info)
    peak = jnp.concatenate([own_peak, other_peak], axis=0)
    total = jnp.concatenate([own_total, other_total], axis=0)
    half = lax.broadcasted_iota(jnp.int32, (group, LANES), 1) < LANES // 2
    part_send[...] = jnp.where(half, peak, total)
    share_part = pltpu.make_async_remote_copy(
        src_ref=part_send,
        dst_ref=part_recv,
        send_sem=pair_send_sem.at[1],
        recv_sem=pair_recv_sem.at[1],
        device_id={"cls": 1 - side},
        device_id_type=MESH,
    )
    share_part.start()
    by_pair = [own_info, own_info, other_info, other_info]
    ids_send[...] = jnp.concatenate(
        [
            jnp.broadcast_to(
                info[:, (2 + place % 2) * cycles : (2 + place % 2) * cycles + 1], (part_dev, LANES)
            )
            for place, info in enumerate(by_pair)
        ],
        axis=0,
    ).astype(jnp.bfloat16)
    mine = pl.ds(pl.multiple_of(me * pairs, pairs), pairs)
    ids_recv[mine, :] = ids_send[...]
    id_copies = []
    for step, peer in enumerate(peers):
        copy = pltpu.make_async_remote_copy(
            src_ref=ids_send,
            dst_ref=ids_recv.at[mine, :],
            send_sem=ids_send_sem.at[step],
            recv_sem=ids_recv_sem.at[step],
            device_id={"dom": peer},
            device_id_type=MESH,
        )
        copy.start()
        id_copies.append(copy)

    def raw_weights(found, peak):
        parts = [jnp.where(live, jnp.exp(value - peak), 0.0) for live, value in found]
        return jnp.concatenate(parts, axis=0).astype(jnp.bfloat16)

    own_raw = raw_weights(own_found, own_peak)
    other_raw = raw_weights(other_found, other_peak)
    raw_weight = jnp.concatenate(
        [jnp.sum(raw.astype(jnp.float32), axis=1, keepdims=True) for raw in (own_raw, other_raw)],
        axis=0,
    )
    filters = raw_weight * jnp.concatenate([info[:, :cycles] for info in by_pair], axis=0)
    pair_sums[:group, :] = jnp.dot(
        own_raw, own_framed[...], preferred_element_type=jnp.float32
    )
    pair_sums[group:, :] = jnp.dot(
        other_raw, other_framed[...], preferred_element_type=jnp.float32
    )
    share_part.wait()
    theirs = part_recv[...]
    theirs = jnp.concatenate([theirs[part_dev:, :], theirs[:part_dev, :]], axis=0)
    their_peak = theirs[:, :1]
    their_total = theirs[:, LANES // 2 : LANES // 2 + 1]
    top = jnp.maximum(peak, their_peak)
    both = total * jnp.exp(peak - top) + their_total * jnp.exp(their_peak - top)
    evidence = top + jnp.log(both)
    corner = lax.broadcasted_iota(jnp.int32, (group, LANES), 1) == lax.broadcasted_iota(
        jnp.int32, (group, LANES), 0
    )
    evidence_row = jnp.sum(jnp.where(corner, evidence, 0.0), axis=0, keepdims=True)
    evidence_ref[...] = evidence_row[:, :part_dev]

    scale = jnp.exp(peak - evidence)
    scale = jnp.concatenate([scale[:part_dev]] * 2 + [scale[part_dev:]] * 2, axis=0)
    filters = filters * scale

    chips = doms // 2
    chip, core = me // 2, lax.rem(me, 2)
    copies = []
    order = [1, chips // 2, *(step for step in range(2, chips) if step != chips // 2), 0]
    for step in order:
        target = lax.rem(chip + step, chips)
        lanes = pl.ds(pl.multiple_of(target * 2 * share, LANES), 2 * share)
        terms = pair_sums[:, lanes] * scale
        for to in range(2):
            here = pl.ds(pl.multiple_of((2 * target + to) * pairs, pairs), pairs)
            stage[here, :] = jnp.concatenate(
                [terms[:, to * share : (to + 1) * share], filters], axis=1
            ).astype(jnp.bfloat16)
        for to in range(2 if step else 1):
            peer = 2 * target + to if step else me + 1 - 2 * core
            copy = pltpu.make_async_remote_copy(
                src_ref=stage.at[pl.ds(pl.multiple_of(peer * pairs, pairs), pairs), :],
                dst_ref=arrived.at[mine, :],
                send_sem=data_send_sem.at[2 * step + to],
                recv_sem=data_recv_sem.at[2 * step + core if step else 0],
                device_id={"dom": peer},
                device_id_type=MESH,
            )
            copy.start()
            copies.append((copy, 2 * step + to, peer))
    arrived[mine, :] = stage[mine, :]

    for copy in id_copies:
        copy.wait()
    ids = jnp.broadcast_to(
        ids_recv[...].astype(jnp.float32)[:, :1], (doms * pairs, class_block)
    )
    column = lax.broadcasted_iota(jnp.int32, (doms * pairs, class_block), 1).astype(jnp.float32)
    chosen_ref[...] = jnp.where(ids == column, 1.0, 0.0).astype(jnp.bfloat16)
    for copy, place, peer in copies:
        copy.wait_send()
        pltpu.make_async_remote_copy(
            src_ref=stage.at[mine, :],
            dst_ref=arrived.at[mine, :],
            send_sem=data_send_sem.at[place],
            recv_sem=data_recv_sem.at[place],
            device_id={"dom": peer},
            device_id_type=MESH,
        ).wait_recv()


def sums_kernel(arrived, chosen, evidence_in, sums_ref, weight_ref, evidence_ref):
    share = sums_ref.shape[1]
    cycles = weight_ref.shape[0]
    contract_first = (((0,), (0,)), ((), ()))
    evidence_ref[...] = evidence_in[...]
    sums = lax.dot_general(
        chosen[...], arrived[...], contract_first, preferred_element_type=jnp.float32
    )
    sums_ref[...] = sums[:, :share]
    filter_sums = lax.dot_general(
        arrived[:, share - cycles :],
        chosen[...],
        contract_first,
        preferred_element_type=jnp.float32,
    )
    weight_ref[...] = filter_sums[cycles:, :]


def paired_shards(images, ctf, inv_noise, classes, candidates):
    doms = lax.axis_size("dom")
    part_dev, features = images.shape
    cycles = ctf.shape[1]
    class_block = classes.shape[0]
    shift = features // ROTATIONS
    group = 2 * part_dev
    rows = ROTATIONS * part_dev
    pairs = TOP_CAND * group
    share = features // doms
    wide = share + cycles
    own_rows = rows + 16
    f32, bf16 = jnp.float32, jnp.bfloat16
    vmem = pl.BlockSpec(memory_space=pltpu.VMEM)
    arrived, chosen, evidence = pl.pallas_call(
        functools.partial(estep_kernel, doms),
        out_shape=(
            jax.ShapeDtypeStruct((doms * pairs, wide), bf16),
            jax.ShapeDtypeStruct((doms * pairs, class_block), bf16),
            jax.ShapeDtypeStruct((1, part_dev), f32),
        ),
        in_specs=[pl.BlockSpec(memory_space=pltpu.HBM)] * 5,
        out_specs=(vmem, vmem, vmem),
        scratch_shapes=[
            pltpu.VMEM((class_block, features), bf16),
            pltpu.VMEM((part_dev, features), bf16),
            pltpu.VMEM((part_dev, cycles), f32),
            pltpu.VMEM((1, cycles), f32),
            pltpu.VMEM((TOP_CAND, part_dev), jnp.int32),
            pltpu.VMEM((own_rows, shift), f32),
            pltpu.VMEM((own_rows, shift), bf16),
            pltpu.VMEM((own_rows, shift), bf16),
            pltpu.VMEM((4, 2 * rows, shift), bf16),
            pltpu.VMEM((rows, features), bf16),
            pltpu.VMEM((rows, features), bf16),
            pltpu.VMEM((group, LANES), f32),
            pltpu.VMEM((group, LANES), f32),
            pltpu.VMEM((pairs, LANES), bf16),
            pltpu.VMEM((doms * pairs, LANES), bf16),
            pltpu.VMEM((doms * pairs, wide), bf16),
            pltpu.VMEM((pairs, features), f32),
            pltpu.SemaphoreType.DMA((5,)),
            pltpu.SemaphoreType.DMA((2,)),
            pltpu.SemaphoreType.DMA((2,)),
            pltpu.SemaphoreType.DMA((doms - 1,)),
            pltpu.SemaphoreType.DMA((doms - 1,)),
            pltpu.SemaphoreType.DMA((doms,)),
            pltpu.SemaphoreType.DMA((doms,)),
        ],
        compiler_params=pltpu.CompilerParams(
            collective_id=0, has_side_effects=True, vmem_limit_bytes=63 * 1024 * 1024
        ),
    )(images, ctf, inv_noise[None, :], candidates.T, classes)
    sums, weight, evidence = pl.pallas_call(
        sums_kernel,
        out_shape=(
            jax.ShapeDtypeStruct((class_block, share), f32),
            jax.ShapeDtypeStruct((cycles, class_block), f32),
            jax.ShapeDtypeStruct((1, part_dev), f32),
        ),
        in_specs=[vmem] * 3,
        out_specs=(vmem, vmem, vmem),
        compiler_params=pltpu.CompilerParams(vmem_limit_bytes=63 * 1024 * 1024),
    )(arrived, chosen, evidence)
    return sums.T, weight.T, evidence.reshape(part_dev)


def pick_plan(images, ctf, inv_noise, classes, candidates):
    doms = lax.axis_size("dom")
    part_dev, features = images.shape
    cycles = ctf.shape[1]
    fits = (
        lax.axis_size("cls") == 2
        and part_dev == 4
        and 2 * cycles == LANES
        and features == ROTATIONS * 2 * LANES
        and doms % 2 == 0
        and (features // doms) % LANES == cycles
        and classes.shape[0] <= 256
    )
    plan = paired_shards if fits else shards
    return plan(images, ctf, inv_noise, classes, candidates)


def solution(mesh):
    in_specs = (
        P(("dom", "cls"), None),
        P(("dom", "cls"), None),
        P(),
        P("cls", None),
        P(("dom", "cls"), None),
    )
    out_specs = (P("dom", "cls"), P("cls", None), P(("dom", "cls")))
    return jax.shard_map(
        pick_plan, mesh=mesh, in_specs=in_specs, out_specs=out_specs, check_vma=False
    )
```
